128 devices in a mesh: seq: 32 (over y, z, core), head: 4 (over x).
Axes of the slice: x: 4, y: 4, z: 4, core: 2. Of those that a mesh axis runs over, the one named last changes fastest.
Arguments:
- query_rows: bfloat16 [16384, 4096], P('seq', 'head'), may hold values from -6 to 6
- key_rows: bfloat16 [16384, 4096], P('seq', 'head'), may hold values from -6 to 6
- value_rows: bfloat16 [16384, 4096], P('seq', 'head'), may hold values from -6 to 6
- log_decay: float32 [32, 16384], P('head', 'seq'), may hold values from -1 to 0, as said below
- norm_gain: float32 [4096], P('head'), may hold values from 0.1 to 1.9
- out_weight: bfloat16 [6144, 4096], P('seq', 'head'), may hold values from -0.09375 to 0.09375
- out_grad: bfloat16 [16384, 6144], P('seq', 'head'), may hold values from -6 to 6
Outputs:
- query_grad: bfloat16 [16384, 4096], P('seq', 'head')
- key_grad: bfloat16 [16384, 4096], P('seq', 'head')
- value_grad: bfloat16 [16384, 4096], P('seq', 'head')
- weight_grad: float32 [6144, 4096], P('seq', 'head')
The draws below stay inside these ranges and needn't reach their ends.
Inputs may be any that keep to these rules, and one draw needn't show every extreme that they name: log_decay holds the logarithm of a decay factor in (0, 1], one per head and position.
All inputs are finite; a program needn't handle non-finite values.
Results may differ from the reference program's by a relative error of at most 0.024.
Values may be sent and summed in bfloat16 or wider, within the bound.
A program may use at most 192 MiB of HBM per device.

```python
import math
import jax
import jax.numpy as jnp
from jax import lax

D = 6144
H = 32
DH = 128
BLOCK = 256
TOK_DEV = 512
TOKENS = 16384
N_SEQ = 32


def draw_log_decay(key, part):
    key = jax.random.fold_in(key, 7)
    keys = jax.random.split(key, 7)
    order = jax.random.permutation(keys[0], H)
    quick_count = H // 2
    quick = (order < quick_count)[:, None]
    quick_rate = jnp.exp(jax.random.uniform(keys[1], (H, 1), jnp.float32, math.log(5.0), math.log(8.5))) / BLOCK
    slow_rate = jnp.exp(jax.random.uniform(keys[2], (H, 1), jnp.float32, math.log(0.1), math.log(0.4))) / TOKENS
    starting_index = jnp.where(quick, quick_rate, slow_rate)
    blocks = TOKENS // BLOCK
    segment_shrink_multiplier = jnp.exp(jax.random.uniform(keys[3], (H, blocks, 1), jnp.float32, math.log(0.5), math.log(2.0)))
    segment_shrink_multiplier = jnp.broadcast_to(segment_shrink_multiplier, (H, blocks, BLOCK)).reshape(H, TOKENS)
    element_shrink_multiplier = jax.random.uniform(keys[4], (H, TOKENS), jnp.float32, 0.5, 1.5)
    element_slots = jax.random.randint(keys[5], (2, 1, 1), 0, TOKENS)
    network_levels = jnp.log(jax.random.uniform(keys[6], (2, H, 1), jnp.float32, 0.5, 0.8))
    element_locations = jnp.arange(TOKENS)[None, None, :]
    segment_span = jnp.sum(jnp.where(element_locations == element_slots, network_levels, 0.0), axis=0)
    return (-(starting_index * segment_shrink_multiplier * element_shrink_multiplier) + segment_span).astype(jnp.float32)


def strengthened(result, rng, source, target, parts, factor):
    def block_of(axis_at):
        return (jnp.arange(result.shape[axis_at]) // (result.shape[axis_at] // parts)).reshape((-1,) + (1,) * (result.ndim - 1 - axis_at))

    near = jax.random.permutation(rng, parts)[block_of(target)]
    far = (block_of(target) + parts // 2) % parts
    return jnp.where((block_of(source) == near) | (block_of(source) == far), factor * result, result)


def levels(key, shape, cuts, smallest, largest):
    factor_of, own = 1.0, jax.random.fold_in(key, 6)
    for axis_at, shards_of in cuts:
        heights = jnp.exp(jax.random.uniform(jax.random.fold_in(own, axis_at), (shards_of,), jnp.float32, smallest / len(cuts), largest / len(cuts)))
        factor_of = factor_of * jnp.repeat(heights, shape[axis_at] // shards_of).reshape([-1 if axis == axis_at else 1 for axis in range(len(shape))])
    return factor_of


def normal_values(key, dims, scale, limit, cuts=(), kind=jnp.bfloat16):
    loudness = levels(key, dims, cuts, -0.22, 0.18) if cuts else 1.0
    drawn = jax.random.normal(key, dims, jnp.float32) * scale * loudness
    return jnp.minimum(jnp.maximum(drawn, -limit), limit).astype(kind)


def heavy_noise(rng, shape, width, reach, cuts, heavy, dtype=jnp.bfloat16):
    entries = width * jax.random.normal(rng, shape, jnp.float32)
    if cuts:
        entries = entries * levels(rng, shape, cuts, -0.22, 0.18)
    return jnp.clip(strengthened(entries, jax.random.fold_in(rng, 3), *heavy), -reach, reach).astype(dtype)


def setup_inputs(seed: int = 0) -> dict:
    streams_of = jax.random.split(jax.random.key(seed), 8)
    return {
        "query_rows": normal_values(streams_of[0], (TOKENS, H * DH), 1.0, 6.0, ((0, 32), (1, 4))),
        "key_rows": normal_values(streams_of[1], (TOKENS, H * DH), 1.0, 6.0, ((0, 32), (1, 4))),
        "value_rows": normal_values(streams_of[2], (TOKENS, H * DH), 1.0, 6.0, ((0, 32), (1, 4))),
        "log_decay": draw_log_decay(jax.random.fold_in(streams_of[7], 71), 0),
        "norm_gain": jnp.clip(1.0 + 0.18 * jax.random.normal(streams_of[4], (H * DH,), jnp.float32), 0.1, 1.9),
        "out_weight": normal_values(streams_of[5], (D, H * DH), (H * DH) ** -0.5, 0.09375, ((0, 32), (1, 4))),
        "out_grad": heavy_noise(streams_of[6], (TOKENS, D), 1.0, 6.0, ((0, 32), (1, 4)), (0, 1, 32, 2.75)),
    }


HIGH = lax.Precision.HIGHEST
EPSILON = 1e-06

def block_attention(query_blk, key_blk, value_blk, decay_blk, carried):
    cumul = jnp.cumsum(decay_blk, axis=0)
    length = decay_blk.shape[0]
    lower = jnp.arange(length)[:, None] >= jnp.arange(length)[None, :]
    spread = jnp.where(lower[:, :, None], cumul[:, None, :] - cumul[None, :, :], 0.0)
    weights = jnp.where(lower[:, :, None], jnp.exp(spread), 0.0)
    scores = jnp.einsum('the,she->tsh', query_blk, key_blk, precision=HIGH) * weights
    output = jnp.einsum('tsh,she->the', scores, value_blk, precision=HIGH)
    output = output + jnp.einsum('the,hef->thf', query_blk * jnp.exp(cumul)[:, :, None], carried, precision=HIGH)
    final = cumul[-1]
    tail = jnp.exp(final[None, :] - cumul)
    updated = jnp.exp(final)[:, None, None] * carried + jnp.einsum('the,thf->hef', key_blk * tail[:, :, None], value_blk, precision=HIGH)
    return (output, updated)

def run_blocks(query_all, key_all, value_all, decay_all, start_state, block):
    count = query_all.shape[0] // block

    def advance(carried, pieces):
        output, updated = block_attention(pieces[0], pieces[1], pieces[2], pieces[3], carried)
        return (updated, output)
    shaped = tuple((tensor.reshape((count, block) + tensor.shape[1:]) for tensor in (query_all, key_all, value_all, decay_all)))
    final, outputs = lax.scan(advance, start_state, shaped)
    return (outputs.reshape(query_all.shape[0], query_all.shape[1], value_all.shape[2]), final)

def normalize(values, gain_row):
    meansq = lax.optimization_barrier(jnp.mean(values * values, axis=-1, keepdims=True))
    scaled = values * lax.rsqrt(meansq + EPSILON)
    return scaled.reshape(values.shape[0], -1) * gain_row

def reference(query_rows, key_rows, value_rows, log_decay, norm_gain, out_weight, out_grad):

    def as_heads(rows):
        return rows.astype(jnp.float32).reshape(TOKENS, H, DH)
    decay_all = log_decay.T
    start_state = jnp.zeros((H, DH, DH), jnp.float32)

    def attention(query_all, key_all, value_all):
        outputs, final = run_blocks(query_all, key_all, value_all, decay_all, start_state, BLOCK)
        return outputs
    attended, attend_back = jax.vjp(attention, as_heads(query_rows), as_heads(key_rows), as_heads(value_rows))

    def norm_only(values):
        return normalize(values, norm_gain)
    normed, norm_back = jax.vjp(norm_only, attended)
    mixed = normed.astype(jnp.bfloat16)
    out_delta = jnp.dot(out_grad, out_weight, preferred_element_type=jnp.float32)
    attended_delta, = norm_back(out_delta)
    query_delta, key_delta, value_delta = attend_back(attended_delta)
    scale = 1.0 / math.sqrt(TOKENS)

    def add_group(total, index):
        first = (index * TOK_DEV).astype(jnp.int32)
        rows_mixed = lax.dynamic_slice_in_dim(mixed, first, TOK_DEV, 0)
        rows_grad = lax.dynamic_slice_in_dim(out_grad, first, TOK_DEV, 0)
        term = lax.dot_general(rows_grad, rows_mixed, (((0,), (0,)), ((), ())), preferred_element_type=jnp.float32) * scale
        rounded = lax.optimization_barrier(term.astype(jnp.bfloat16))
        return (total + rounded.astype(jnp.float32), None)
    weight_grad, unused = lax.scan(add_group, jnp.zeros((D, H * DH), jnp.float32), jnp.arange(N_SEQ).astype(jnp.int32))
    shape_rows = (TOKENS, H * DH)
    return (query_delta.reshape(shape_rows).astype(jnp.bfloat16), key_delta.reshape(shape_rows).astype(jnp.bfloat16), value_delta.reshape(shape_rows).astype(jnp.bfloat16), weight_grad)
```

```python
import jax
import jax.numpy as jnp
from jax import lax
from jax.experimental import pallas as pl
from jax.experimental.pallas import tpu as pltpu
from jax.sharding import PartitionSpec as P

MESH = pl.DeviceIdType.MESH
BF = jnp.bfloat16
F32 = jnp.float32
HIGH = lax.Precision.HIGHEST
EPSILON = 1e-06

ROWS = 512
HEADS = 8
WIDE = 128
COLS = 1024
UNIT = 192
HALF = 96
QUART = 48
SPAN = 768
BLK = 256
SCALE = 1.0 / 128.0

S_SIB = 0
S_X = 1
S_W = 7
S_MIX = 23
S_OD = 24
S_RS = 25
S_F1 = 41
S_F2 = 48
S_F3 = 51
S_B1 = 58
S_B2 = 65
S_B3 = 68
S_ALL = 75


def dot(a, b):
    return lax.dot_general(a, b, (((1,), (0,)), ((), ())), preferred_element_type=F32)


def dot_t0(a, b):
    return lax.dot_general(a, b, (((0,), (0,)), ((), ())), preferred_element_type=F32)


def dot_t1(a, b):
    return lax.dot_general(a, b, (((1,), (1,)), ((), ())), preferred_element_type=F32)


def kernel(
    q, k, v, ld, gain, w, g,
    dq, dk, dv, dw,
    OG, OGS, WB, ACC, XO, XI, MX, DW, R1, R2, R3, R4,
    PB, ATT, DA, CC, RN, CR,
    ST, STI, RT, RTI, EN, ENT, LL, EP,
    GS, GSI, GR, GRI, GO, GG,
    ss, rs,
):
    me = lax.axis_index("seq")
    x = lax.axis_index("head")
    y = lax.div(me, 8)
    grp = lax.rem(me, 8)
    z = lax.div(grp, 2)
    c = lax.rem(me, 2)
    o = 1 - c

    def turn(a, d):
        return lax.rem(a + d, 4)

    yn, yo, yp = turn(y, 1), turn(y, 2), turn(y, 3)
    zn, zo, zp = turn(z, 1), turn(z, 2), turn(z, 3)
    xn, xo, xp = turn(x, 1), turn(x, 2), turn(x, 3)

    def at(yy, zz, cc):
        return ((yy * 4 + zz) * 2 + cc, x)

    YN, YP, ZN, ZP = at(yn, z, c), at(yp, z, c), at(y, zn, c), at(y, zp, c)
    XN, XP = (me, xn), (me, xp)
    SIB = at(y, z, o)

    def mate(d):
        p = lax.rem(grp + d, 8)
        return p, (y * 8 + p, x)

    live = []

    def put(i, src, dst, dev):
        copy = pltpu.make_async_remote_copy(
            src_ref=src,
            dst_ref=dst,
            send_sem=ss.at[i],
            recv_sem=rs.at[i],
            device_id=dev,
            device_id_type=MESH,
        )
        copy.start()
        live.append(copy)
        return copy

    barrier = pltpu.get_barrier_semaphore()
    partners = [mate(d)[1] for d in range(1, 8)]
    partners += [at(turn(y, d), z, c) for d in (1, 2, 3)]
    partners += [XN, XP]
    for dev in partners:
        pl.semaphore_signal(barrier, inc=1, device_id=dev, device_id_type=MESH)
    pl.semaphore_wait(barrier, len(partners))

    own_rows = pl.ds(pl.multiple_of(c * ROWS, ROWS), ROWS)
    sib_rows = pl.ds(pl.multiple_of(o * ROWS, ROWS), ROWS)
    rows_a, rows_b = pl.ds(0, HALF), pl.ds(HALF, HALF)
    a_lo, a_hi = pl.ds(0, QUART), pl.ds(QUART, QUART)
    b_lo, b_hi = pl.ds(HALF, QUART), pl.ds(HALF + QUART, QUART)

    WB[y, z] = w[...]
    wa0 = put(S_W + 0, WB.at[y, z, rows_a], WB.at[y, z, rows_a], YN)
    wa1 = put(S_W + 1, WB.at[y, z, rows_a], WB.at[y, z, rows_a], YP)
    wb0 = put(S_W + 8, WB.at[y, z, rows_b], WB.at[y, z, rows_b], ZN)
    wb1 = put(S_W + 9, WB.at[y, z, rows_b], WB.at[y, z, rows_b], ZP)

    for part in range(4):
        r = pl.ds(part * 128, 128)
        rows = g[r, :]
        even = jnp.concatenate(
            [rows[:, (2 * i) * UNIT : (2 * i + 1) * UNIT] for i in range(4)], axis=1
        )
        odd = jnp.concatenate(
            [rows[:, (2 * i + 1) * UNIT : (2 * i + 2) * UNIT] for i in range(4)], axis=1
        )
        mine = jnp.where(c == 0, even, odd)
        other = jnp.where(c == 0, odd, even)
        OG[x, pl.ds(pl.multiple_of(c * ROWS + part * 128, 128), 128), :] = mine
        OGS[r, :] = other
    sib = put(S_SIB, OGS, OG.at[x, own_rows], SIB)
    xr0 = put(S_X + 0, OG.at[x, own_rows], OG.at[x, own_rows], XN)
    xl1 = put(S_X + 3, OG.at[x, own_rows], OG.at[x, own_rows], XP)

    row_i = lax.broadcasted_iota(jnp.int32, (ROWS, ROWS), 0)
    col_i = lax.broadcasted_iota(jnp.int32, (ROWS, ROWS), 1)
    upper = (row_i <= col_i).astype(F32)
    lower = (row_i >= col_i).astype(F32)
    by_rows = lax.dot_general(
        ld[...], upper, (((1,), (0,)), ((), ())), precision=HIGH, preferred_element_type=F32
    )
    by_cols = lax.dot_general(
        lower, ld[...], (((1,), (1,)), ((), ())), precision=HIGH, preferred_element_type=F32
    )
    for h in range(HEADS):
        CR[h] = by_rows[h : h + 1, :]
        CC[h] = by_cols[:, h : h + 1]

    sib.wait_recv()
    xl0 = put(S_X + 2, OG.at[x, sib_rows], OG.at[x, sib_rows], XP)
    xr1 = put(S_X + 1, OG.at[x, sib_rows], OG.at[x, sib_rows], XN)

    def head_cols(h):
        return pl.ds(pl.multiple_of(h * WIDE, WIDE), WIDE)

    def decays(h, tb, sb):
        cc = CC[h, pl.ds(tb * BLK, BLK), :]
        cr = CR[h, :, pl.ds(sb * BLK, BLK)]
        grown = jnp.exp(cc - cr)
        if tb == sb:
            t = lax.broadcasted_iota(jnp.int32, (BLK, BLK), 0)
            s = lax.broadcasted_iota(jnp.int32, (BLK, BLK), 1)
            grown = jnp.where(t >= s, grown, 0.0)
        return grown

    def blk(b):
        return pl.ds(b * BLK, BLK)

    row16 = lax.broadcasted_iota(jnp.int32, (16, WIDE), 0)

    def split3(row):
        hi = row.astype(BF).astype(F32)
        mid = (row - hi).astype(BF).astype(F32)
        lo = (row - hi - mid).astype(BF).astype(F32)
        full = jnp.where(
            row16 == 0, hi, jnp.where(row16 == 1, mid, jnp.where(row16 == 2, lo, 0.0))
        )
        return full.astype(BF)

    def join3(block):
        return jnp.sum(block.astype(F32), axis=0, keepdims=True)

    def forward_head(h, _):
        hs = head_cols(h)
        for tb in range(2):
            out = jnp.zeros((BLK, WIDE), F32)
            for sb in range(tb + 1):
                scores = dot_t1(q[blk(tb), hs], k[blk(sb), hs])
                p = (scores * decays(h, tb, sb)).astype(BF)
                PB[h, blk(tb), blk(sb)] = p
                out = out + dot(p, v[blk(sb), hs])
            ATT[blk(tb), hs] = out
        total = CR[h, :, pl.ds(ROWS - WIDE, WIDE)][:, WIDE - 1 : WIDE]
        kd = (k[:, hs].astype(F32) * jnp.exp(total - CC[h])).astype(BF)
        ST[h, pl.ds(0, WIDE), :] = dot_t0(kd, v[:, hs]).astype(BF)
        ST[h, pl.ds(WIDE, 16), :] = split3(jnp.broadcast_to(total, (1, WIDE)))
        return 0

    lax.fori_loop(0, 4, forward_head, 0)

    wa0.wait_recv()
    wa2 = put(S_W + 2, WB.at[yp, z, a_lo], WB.at[yp, z, a_lo], YN)
    wa1.wait_recv()
    wa3 = put(S_W + 3, WB.at[yn, z, a_hi], WB.at[yn, z, a_hi], YP)
    wb0.wait_recv()
    wb2 = put(S_W + 10, WB.at[y, zp, b_lo], WB.at[y, zp, b_lo], ZN)
    wb1.wait_recv()
    wb3 = put(S_W + 11, WB.at[y, zn, b_hi], WB.at[y, zn, b_hi], ZP)

    lax.fori_loop(4, 8, forward_head, 0)

    STI[grp] = ST[grp]
    f1 = []
    for d in range(1, 8):
        p, dev = mate(d)
        f1.append(put(S_F1 + d - 1, ST.at[p], STI.at[grp], dev))

    wa2.wait_recv()
    wa3.wait_recv()
    wa4 = put(S_W + 4, WB.at[:, z, rows_a], WB.at[:, z, rows_a], ZN)
    wa5 = put(S_W + 5, WB.at[:, z, rows_a], WB.at[:, z, rows_a], ZP)
    wb2.wait_recv()
    wb3.wait_recv()
    wb4 = put(S_W + 12, WB.at[y, :, rows_b], WB.at[y, :, rows_b], YN)
    wb5 = put(S_W + 13, WB.at[y, :, rows_b], WB.at[y, :, rows_b], YP)

    for copy in f1:
        copy.wait_recv()

    def chain(i, carry):
        state, logs = carry
        log_i = join3(STI[i, pl.ds(WIDE, 16), :])
        LL[i] = state
        EP[i] = logs
        state = jnp.exp(log_i) * state + STI[i, pl.ds(0, WIDE), :].astype(F32)
        return state, logs + log_i

    row_state, row_logs = lax.fori_loop(
        0, 8, chain, (jnp.zeros((WIDE, WIDE), F32), jnp.zeros((1, WIDE), F32))
    )
    RT[pl.ds(0, WIDE), :] = row_state.astype(BF)
    RT[pl.ds(WIDE, 16), :] = split3(row_logs)
    RTI[y] = RT[...]
    f2 = [
        put(S_F2 + d - 1, RT, RTI.at[y], at(turn(y, d), z, c)) for d in (1, 2, 3)
    ]
    for copy in f2:
        copy.wait_recv()
    carried = jnp.zeros((WIDE, WIDE), F32)
    for yy in range(3):
        grown = jnp.exp(join3(RTI[yy, pl.ds(WIDE, 16), :])) * carried
        grown = grown + RTI[yy, pl.ds(0, WIDE), :].astype(F32)
        carried = jnp.where(yy < y, grown, carried)

    def enter(i, _):
        EN[i] = (LL[i] + jnp.exp(EP[i]) * carried).astype(BF)
        return 0

    lax.fori_loop(0, 8, enter, 0)
    ENT[grp] = EN[grp]
    f3 = []
    for d in range(1, 8):
        p, dev = mate(d)
        f3.append(put(S_F3 + d - 1, EN.at[p], ENT.at[grp], dev))
    for copy in f3:
        copy.wait_recv()

    def attend_head(h, _):
        hs = head_cols(h)
        att = ATT[:, hs] + jnp.exp(CC[h]) * dot(q[:, hs], ENT[h])
        r = lax.rsqrt(jnp.mean(att * att, axis=-1, keepdims=True) + EPSILON)
        scaled = att * r
        ATT[:, hs] = scaled
        RN[h] = r
        MX[c, :, hs] = (scaled * gain[:, hs]).astype(BF)
        return 0

    lax.fori_loop(0, HEADS, attend_head, 0)
    mix = put(S_MIX, MX.at[c], MX.at[c], SIB)

    wa4.wait_recv()
    wa6 = put(S_W + 6, WB.at[:, zp, a_lo], WB.at[:, zp, a_lo], ZN)
    wa5.wait_recv()
    wa7 = put(S_W + 7, WB.at[:, zn, a_hi], WB.at[:, zn, a_hi], ZP)
    wb4.wait_recv()
    wb6 = put(S_W + 14, WB.at[yp, :, b_lo], WB.at[yp, :, b_lo], YN)
    wb5.wait_recv()
    wb7 = put(S_W + 15, WB.at[yn, :, b_hi], WB.at[yn, :, b_hi], YP)

    def weight_term(xx):
        def tile(i, _):
            pair = lax.div(i, 2)
            n = lax.rem(i, 2)
            ms = pl.ds(pl.multiple_of(pair * 384, 384), 384)
            ns = pl.ds(pl.multiple_of(n * 512, 512), 512)
            term = dot_t0(OG[xx, pl.ds(0, ROWS), ms], MX[0, :, ns])
            term = term + dot_t0(OG[xx, pl.ds(ROWS, ROWS), ms], MX[1, :, ns])
            DW[xx, pl.ds(2 * pair, 2), :, ns] = term.reshape(2, UNIT, 512).astype(BF)
            return 0

        lax.fori_loop(0, 4, tile, 0)

    def delta_term(xx, first, half):
        def tile(i, _):
            m = lax.div(i, 2)
            n = lax.rem(i, 2)
            ms = pl.ds(pl.multiple_of(half * ROWS + m * BLK, BLK), BLK)
            ns = pl.ds(pl.multiple_of(n * 512, 512), 512)
            term = dot(OG[xx, ms, :], WB[xx, :, :, ns].reshape(SPAN, 512))
            if first:
                ACC[ms, ns] = term
            else:
                ACC[ms, ns] += term
            return 0

        lax.fori_loop(0, 4, tile, 0)

    mix.wait_recv()
    weight_term(x)

    xr0.wait_recv()
    xr2 = put(S_X + 4, OG.at[xp, own_rows], OG.at[xp, own_rows], XN)
    xl0.wait_recv()
    xl2 = put(S_X + 5, OG.at[xn, sib_rows], OG.at[xn, sib_rows], XP)

    for copy in (wa6, wa7, wb6, wb7):
        copy.wait_recv()
    delta_term(x, True, o)
    delta_term(x, True, c)
    xr1.wait_recv()
    xl1.wait_recv()
    for xx in (xp, xn):
        weight_term(xx)
        delta_term(xx, False, o)
        delta_term(xx, False, c)
    xr2.wait_recv()
    xl2.wait_recv()
    weight_term(xo)

    ra0 = put(S_RS + 0, DW.at[:, zo, a_lo], R1.at[0, 0], ZN)
    ra1 = put(S_RS + 1, DW.at[:, zo, a_hi], R1.at[0, 1], ZP)
    rb0 = put(S_RS + 8, DW.at[yo, :, b_lo], R1.at[1, 0], YN)
    rb1 = put(S_RS + 9, DW.at[yo, :, b_hi], R1.at[1, 1], YP)

    delta_term(xo, False, o)
    XO[...] = ACC[sib_rows, :].astype(BF)
    od = put(S_OD, XO, XI, SIB)
    delta_term(xo, False, c)
    od.wait_recv()

    def norm_back_head(h, _):
        hs = head_cols(h)
        delta = ACC[own_rows, hs] + XI[:, hs].astype(F32)
        scaled = ATT[:, hs]
        gg = delta * gain[:, hs]
        da = RN[h] * (gg - scaled * jnp.mean(gg * scaled, axis=-1, keepdims=True))
        da = da.astype(BF)
        DA[:, hs] = da
        qd = (q[:, hs].astype(F32) * jnp.exp(CC[h])).astype(BF)
        GS[h] = dot_t0(qd, da).astype(BF)
        return 0

    lax.fori_loop(0, HEADS, norm_back_head, 0)

    GSI[grp] = GS[grp]
    b1 = []
    for d in range(1, 8):
        p, dev = mate(d)
        b1.append(put(S_B1 + d - 1, GS.at[p], GSI.at[grp], dev))

    def add_to(target, more):
        return (target.astype(F32) + more.astype(F32)).astype(BF)

    ra0.wait_recv()
    for i in range(4):
        DW[i, zn, a_lo] = add_to(DW[i, zn, a_lo], R1[0, 0, i])
    ra2 = put(S_RS + 2, DW.at[:, zn, rows_a], R2.at[0, 0], ZN)
    ra1.wait_recv()
    for i in range(4):
        DW[i, zp, a_hi] = add_to(DW[i, zp, a_hi], R1[0, 1, i])
    ra3 = put(S_RS + 3, DW.at[:, zp, rows_a], R2.at[0, 1], ZP)
    rb0.wait_recv()
    for i in range(4):
        DW[yn, i, b_lo] = add_to(DW[yn, i, b_lo], R1[1, 0, i])
    rb2 = put(S_RS + 10, DW.at[yn, :, rows_b], R2.at[1, 0], YN)
    rb1.wait_recv()
    for i in range(4):
        DW[yp, i, b_hi] = add_to(DW[yp, i, b_hi], R1[1, 1, i])
    rb3 = put(S_RS + 11, DW.at[yp, :, rows_b], R2.at[1, 1], YP)

    for copy in b1:
        copy.wait_recv()

    def chain_back(n, carry):
        i = 7 - n
        state, logs = carry
        log_i = join3(STI[i, pl.ds(WIDE, 16), :])
        LL[i] = state
        EP[i] = logs
        state = jnp.exp(log_i) * state + GSI[i].astype(F32)
        return state, logs + log_i

    row_back, _ = lax.fori_loop(
        0, 8, chain_back, (jnp.zeros((WIDE, WIDE), F32), jnp.zeros((1, WIDE), F32))
    )
    GR[...] = row_back.astype(BF)
    GRI[y] = GR[...]
    b2 = [
        put(S_B2 + d - 1, GR, GRI.at[y], at(turn(y, d), z, c)) for d in (1, 2, 3)
    ]

    def local_back_head(h, _):
        hs = head_cols(h)
        dk_blk = [None, None]
        dv_blk = [None, None]
        for tb in range(2):
            da = DA[blk(tb), hs]
            out = jnp.exp(CC[h, blk(tb), :]) * dot_t1(da, ENT[h])
            for sb in range(tb + 1):
                dp = (dot_t1(da, v[blk(sb), hs]) * decays(h, tb, sb)).astype(BF)
                out = out + dot(dp, k[blk(sb), hs])
                k_term = dot_t0(dp, q[blk(tb), hs])
                v_term = dot_t0(PB[h, blk(tb), blk(sb)], da)
                dk_blk[sb] = k_term if dk_blk[sb] is None else dk_blk[sb] + k_term
                dv_blk[sb] = v_term if dv_blk[sb] is None else dv_blk[sb] + v_term
            dq[blk(tb), hs] = out.astype(BF)
        for sb in range(2):
            ACC[blk(sb), hs] = dk_blk[sb]
            ACC[blk(2 + sb), hs] = dv_blk[sb]
        return 0

    lax.fori_loop(0, 4, local_back_head, 0)

    for copy in b2:
        copy.wait_recv()
    carried_back = jnp.zeros((WIDE, WIDE), F32)
    for yy in (3, 2, 1):
        grown = jnp.exp(join3(RTI[yy, pl.ds(WIDE, 16), :])) * carried_back
        grown = grown + GRI[yy].astype(F32)
        carried_back = jnp.where(yy > y, grown, carried_back)

    def leave(i, _):
        GO[i] = (LL[i] + jnp.exp(EP[i]) * carried_back).astype(BF)
        return 0

    lax.fori_loop(0, 8, leave, 0)
    GG[grp] = GO[grp]
    b3 = []
    for d in range(1, 8):
        p, dev = mate(d)
        b3.append(put(S_B3 + d - 1, GO.at[p], GG.at[grp], dev))

    lax.fori_loop(4, 8, local_back_head, 0)

    ra2.wait_recv()
    ra3.wait_recv()
    for i in range(4):
        DW[i, z, rows_a] = (
            DW[i, z, rows_a].astype(F32) + R2[0, 0, i].astype(F32) + R2[0, 1, i].astype(F32)
        ).astype(BF)
    ra4 = put(S_RS + 4, DW.at[yo, z, a_lo], R3.at[0, 0], YN)
    ra5 = put(S_RS + 5, DW.at[yo, z, a_hi], R3.at[0, 1], YP)
    rb2.wait_recv()
    rb3.wait_recv()
    for i in range(4):
        DW[y, i, rows_b] = (
            DW[y, i, rows_b].astype(F32) + R2[1, 0, i].astype(F32) + R2[1, 1, i].astype(F32)
        ).astype(BF)
    rb4 = put(S_RS + 12, DW.at[y, zo, b_lo], R3.at[1, 0], ZN)
    rb5 = put(S_RS + 13, DW.at[y, zo, b_hi], R3.at[1, 1], ZP)

    for copy in b3:
        copy.wait_recv()

    def last_head(h, _):
        hs = head_cols(h)
        total = CR[h, :, pl.ds(ROWS - WIDE, WIDE)][:, WIDE - 1 : WIDE]
        tail = jnp.exp(total - CC[h])
        dk[:, hs] = (ACC[pl.ds(0, ROWS), hs] + tail * dot_t1(v[:, hs], GG[h])).astype(BF)
        dv[:, hs] = (ACC[pl.ds(ROWS, ROWS), hs] + tail * dot(k[:, hs], GG[h])).astype(BF)
        return 0

    lax.fori_loop(0, 4, last_head, 0)

    ra4.wait_recv()
    DW[yn, z, a_lo] = add_to(DW[yn, z, a_lo], R3[0, 0])
    ra6 = put(S_RS + 6, DW.at[yn, z, rows_a], R4.at[0, 0], YN)
    ra5.wait_recv()
    DW[yp, z, a_hi] = add_to(DW[yp, z, a_hi], R3[0, 1])
    ra7 = put(S_RS + 7, DW.at[yp, z, rows_a], R4.at[0, 1], YP)
    rb4.wait_recv()
    DW[y, zn, b_lo] = add_to(DW[y, zn, b_lo], R3[1, 0])
    rb6 = put(S_RS + 14, DW.at[y, zn, rows_b], R4.at[1, 0], ZN)
    rb5.wait_recv()
    DW[y, zp, b_hi] = add_to(DW[y, zp, b_hi], R3[1, 1])
    rb7 = put(S_RS + 15, DW.at[y, zp, rows_b], R4.at[1, 1], ZP)

    lax.fori_loop(4, 8, last_head, 0)

    ra6.wait_recv()
    ra7.wait_recv()
    dw[rows_a, :] = (
        DW[y, z, rows_a].astype(F32) + R4[0, 0].astype(F32) + R4[0, 1].astype(F32)
    ) * SCALE
    rb6.wait_recv()
    rb7.wait_recv()
    dw[rows_b, :] = (
        DW[y, z, rows_b].astype(F32) + R4[1, 0].astype(F32) + R4[1, 1].astype(F32)
    ) * SCALE

    for copy in live:
        copy.wait_send()


def body(query_rows, key_rows, value_rows, log_decay, norm_gain, out_weight, out_grad):
    vm = pltpu.VMEM
    scratch = [
        vm((4, 2 * ROWS, SPAN), BF),
        vm((ROWS, SPAN), BF),
        vm((4, 4, UNIT, COLS), BF),
        vm((2 * ROWS, COLS), F32),
        vm((ROWS, COLS), BF),
        vm((ROWS, COLS), BF),
        vm((2, ROWS, COLS), BF),
        vm((4, 4, UNIT, COLS), BF),
        vm((2, 2, 4, QUART, COLS), BF),
        vm((2, 2, 4, HALF, COLS), BF),
        vm((2, 2, QUART, COLS), BF),
        vm((2, 2, HALF, COLS), BF),
        vm((HEADS, ROWS, ROWS), BF),
        vm((ROWS, COLS), F32),
        vm((ROWS, COLS), BF),
        vm((HEADS, ROWS, 1), F32),
        vm((HEADS, ROWS, 1), F32),
        vm((HEADS, 1, ROWS), F32),
        vm((8, WIDE + 16, WIDE), BF),
        vm((8, WIDE + 16, WIDE), BF),
        vm((WIDE + 16, WIDE), BF),
        vm((4, WIDE + 16, WIDE), BF),
        vm((8, WIDE, WIDE), BF),
        vm((8, WIDE, WIDE), BF),
        vm((8, WIDE, WIDE), F32),
        vm((8, 1, WIDE), F32),
        vm((8, WIDE, WIDE), BF),
        vm((8, WIDE, WIDE), BF),
        vm((WIDE, WIDE), BF),
        vm((4, WIDE, WIDE), BF),
        vm((8, WIDE, WIDE), BF),
        vm((8, WIDE, WIDE), BF),
        pltpu.SemaphoreType.DMA((S_ALL,)),
        pltpu.SemaphoreType.DMA((S_ALL,)),
    ]
    spec = pl.BlockSpec(memory_space=pltpu.VMEM)
    return pl.pallas_call(
        kernel,
        out_shape=(
            jax.ShapeDtypeStruct((ROWS, COLS), BF),
            jax.ShapeDtypeStruct((ROWS, COLS), BF),
            jax.ShapeDtypeStruct((ROWS, COLS), BF),
            jax.ShapeDtypeStruct((UNIT, COLS), F32),
        ),
        in_specs=[spec] * 7,
        out_specs=(spec,) * 4,
        scratch_shapes=scratch,
        compiler_params=pltpu.CompilerParams(
            collective_id=0, has_side_effects=True, vmem_limit_bytes=62 * 2**20
        ),
    )(
        query_rows,
        key_rows,
        value_rows,
        log_decay,
        norm_gain.reshape(1, COLS),
        out_weight,
        out_grad,
    )


def solution(mesh):
    both = P("seq", "head")
    return jax.shard_map(
        body,
        mesh=mesh,
        in_specs=(both, both, both, P("head", "seq"), P("head"), both, both),
        out_specs=(both, both, both, both),
        check_vma=False,
    )
```

```python
import jax
import jax.numpy as jnp
from jax import lax
from jax.experimental import pallas as pl
from jax.experimental.pallas import tpu as pltpu
from jax.sharding import PartitionSpec as P

MESH = pl.DeviceIdType.MESH
BF = jnp.bfloat16
F32 = jnp.float32
HIGH = lax.Precision.HIGHEST
EPSILON = 1e-06

ROWS = 512
HEADS = 8
WIDE = 128
COLS = 1024
UNIT = 192
HALF = 96
QUART = 48
SPAN = 768
BLK = 256
SCALE = 1.0 / 128.0

S_SIB = 0
S_X = 1
S_MIX = 7
S_OD = 8
S_W = 10
S_A1 = 42
S_A2 = 50
S_RS = 58
S_F1 = 70
S_F2 = 77
S_F3 = 80
S_B1 = 87
S_B2 = 94
S_B3 = 97
S_ALL = 104


def dot(a, b):
    return lax.dot_general(a, b, (((1,), (0,)), ((), ())), preferred_element_type=F32)


def dot_t0(a, b):
    return lax.dot_general(a, b, (((0,), (0,)), ((), ())), preferred_element_type=F32)


def dot_t1(a, b):
    return lax.dot_general(a, b, (((1,), (1,)), ((), ())), preferred_element_type=F32)


def kernel(
    q, k, v, ld, gain, w, g,
    dq, dk, dv, dw,
    OG, OGS, WB, ACC, XO, XI, MX, DW, R1, R2, R3, R4, R1B, R2B,
    PB, ATT, DA, CC, RN, CR,
    ST, STI, RT, RTI, EN, ENT, LL, EP,
    GS, GSI, GR, GRI, GO, GG,
    ss, rs,
):
    me = lax.axis_index("seq")
    x = lax.axis_index("head")
    y = lax.div(me, 8)
    grp = lax.rem(me, 8)
    z = lax.div(grp, 2)
    c = lax.rem(me, 2)
    o = 1 - c

    def turn(a, d):
        return lax.rem(a + d, 4)

    yn, yo, yp = turn(y, 1), turn(y, 2), turn(y, 3)
    zn, zo, zp = turn(z, 1), turn(z, 2), turn(z, 3)
    xn, xo, xp = turn(x, 1), turn(x, 2), turn(x, 3)

    def at(yy, zz, cc):
        return ((yy * 4 + zz) * 2 + cc, x)

    YN, YP, ZN, ZP = at(yn, z, c), at(yp, z, c), at(y, zn, c), at(y, zp, c)
    XN, XP = (me, xn), (me, xp)
    SIB = at(y, z, o)

    def mate(d):
        p = lax.rem(grp + d, 8)
        return p, (y * 8 + p, x)

    live = []

    def make(i, src, dst, dev):
        return pltpu.make_async_remote_copy(
            src_ref=src,
            dst_ref=dst,
            send_sem=ss.at[i],
            recv_sem=rs.at[i],
            device_id=dev,
            device_id_type=MESH,
        )

    def put(i, src, dst, dev):
        copy = make(i, src, dst, dev)
        copy.start()
        live.append(copy)
        return copy

    def same(i, ref, dev):
        return put(i, ref, ref, dev)

    barrier = pltpu.get_barrier_semaphore()
    partners = [mate(d)[1] for d in range(1, 8)]
    partners += [at(turn(y, d), z, c) for d in (1, 2, 3)]
    partners += [XN, XP]
    for dev in partners:
        pl.semaphore_signal(barrier, inc=1, device_id=dev, device_id_type=MESH)
    pl.semaphore_wait(barrier, len(partners))

    own_rows = pl.ds(pl.multiple_of(c * ROWS, ROWS), ROWS)
    sib_rows = pl.ds(pl.multiple_of(o * ROWS, ROWS), ROWS)

    WB[y, z] = w[...].reshape(2, 2, QUART, COLS)
    wy0 = same(S_W + 0, WB.at[y, z], YN)
    wy1 = same(S_W + 1, WB.at[y, z], YP)
    wz0 = same(S_W + 2, WB.at[y, z], ZN)
    wz1 = same(S_W + 3, WB.at[y, z], ZP)

    for part in range(4):
        r = pl.ds(part * 128, 128)
        rows = g[r, :]
        even = jnp.concatenate(
            [rows[:, (2 * i) * UNIT : (2 * i + 1) * UNIT] for i in range(4)], axis=1
        )
        odd = jnp.concatenate(
            [rows[:, (2 * i + 1) * UNIT : (2 * i + 2) * UNIT] for i in range(4)], axis=1
        )
        mine = jnp.where(c == 0, even, odd)
        other = jnp.where(c == 0, odd, even)
        OG[x, pl.ds(pl.multiple_of(c * ROWS + part * 128, 128), 128), :] = mine
        OGS[r, :] = other
    sib = put(S_SIB, OGS, OG.at[x, own_rows], SIB)
    xr0 = put(S_X + 0, OG.at[x, own_rows], OG.at[x, own_rows], XN)
    xl1 = put(S_X + 3, OG.at[x, own_rows], OG.at[x, own_rows], XP)

    row_i = lax.broadcasted_iota(jnp.int32, (ROWS, ROWS), 0)
    col_i = lax.broadcasted_iota(jnp.int32, (ROWS, ROWS), 1)
    upper = (row_i <= col_i).astype(F32)
    lower = (row_i >= col_i).astype(F32)
    by_rows = lax.dot_general(
        ld[...], upper, (((1,), (0,)), ((), ())), precision=HIGH, preferred_element_type=F32
    )
    by_cols = lax.dot_general(
        lower, ld[...], (((1,), (1,)), ((), ())), precision=HIGH, preferred_element_type=F32
    )
    for h in range(HEADS):
        CR[h] = by_rows[h : h + 1, :]
        CC[h] = by_cols[:, h : h + 1]

    sib.wait_recv()
    xl0 = put(S_X + 2, OG.at[x, sib_rows], OG.at[x, sib_rows], XP)
    xr1 = put(S_X + 1, OG.at[x, sib_rows], OG.at[x, sib_rows], XN)

    def head_cols(h):
        return pl.ds(pl.multiple_of(h * WIDE, WIDE), WIDE)

    def decays(h, tb, sb):
        cc = CC[h, pl.ds(tb * BLK, BLK), :]
        cr = CR[h, :, pl.ds(sb * BLK, BLK)]
        grown = jnp.exp(cc - cr)
        if tb == sb:
            t = lax.broadcasted_iota(jnp.int32, (BLK, BLK), 0)
            s = lax.broadcasted_iota(jnp.int32, (BLK, BLK), 1)
            grown = jnp.where(t >= s, grown, 0.0)
        return grown

    def blk(b):
        return pl.ds(b * BLK, BLK)

    row16 = lax.broadcasted_iota(jnp.int32, (16, WIDE), 0)

    def split3(row):
        hi = row.astype(BF).astype(F32)
        mid = (row - hi).astype(BF).astype(F32)
        lo = (row - hi - mid).astype(BF).astype(F32)
        full = jnp.where(
            row16 == 0, hi, jnp.where(row16 == 1, mid, jnp.where(row16 == 2, lo, 0.0))
        )
        return full.astype(BF)

    def join3(block):
        return jnp.sum(block.astype(F32), axis=0, keepdims=True)

    def forward_head(h):
        hs = head_cols(h)
        for tb in range(2):
            out = jnp.zeros((BLK, WIDE), F32)
            for sb in range(tb + 1):
                scores = dot_t1(q[blk(tb), hs], k[blk(sb), hs])
                p = (scores * decays(h, tb, sb)).astype(BF)
                PB[h, blk(tb), blk(sb)] = p
                out = out + dot(p, v[blk(sb), hs])
            ATT[blk(tb), hs] = out
        total = CR[h, :, pl.ds(ROWS - WIDE, WIDE)][:, WIDE - 1 : WIDE]
        kd = (k[:, hs].astype(F32) * jnp.exp(total - CC[h])).astype(BF)
        ST[h, pl.ds(0, WIDE), :] = dot_t0(kd, v[:, hs]).astype(BF)
        ST[h, pl.ds(WIDE, 16), :] = split3(jnp.broadcast_to(total, (1, WIDE)))

    def first(d):
        p, dev = mate(d)
        return make(S_F1 + d - 1, ST.at[p], STI.at[grp], dev)

    def forward_step(d, _):
        forward_head(lax.rem(grp + d, 8))
        first(d).start()
        return 0

    lax.fori_loop(1, 8, forward_step, 0)
    forward_head(grp)
    STI[grp] = ST[grp]
    f1 = [first(d) for d in range(1, 8)]
    live += f1

    wy0.wait_recv()
    wyf0 = same(S_W + 4, WB.at[yp, z, :, 0], YN)
    wyp0 = same(S_W + 5, WB.at[yp, z, 0], ZN)
    wyp1 = same(S_W + 6, WB.at[yp, z, 0], ZP)
    wy1.wait_recv()
    wyf1 = same(S_W + 7, WB.at[yn, z, :, 1], YP)
    wyn0 = same(S_W + 8, WB.at[yn, z, 0], ZN)
    wyn1 = same(S_W + 9, WB.at[yn, z, 0], ZP)
    wz0.wait_recv()
    wzf0 = same(S_W + 10, WB.at[y, zp, :, 0], ZN)
    wzp0 = same(S_W + 11, WB.at[y, zp, 1], YN)
    wzp1 = same(S_W + 12, WB.at[y, zp, 1], YP)
    wz1.wait_recv()
    wzf1 = same(S_W + 13, WB.at[y, zn, :, 1], ZP)
    wzn0 = same(S_W + 14, WB.at[y, zn, 1], YN)
    wzn1 = same(S_W + 15, WB.at[y, zn, 1], YP)

    for copy in f1:
        copy.wait_recv()

    def chain(i, carry):
        state, logs = carry
        log_i = join3(STI[i, pl.ds(WIDE, 16), :])
        LL[i] = state
        EP[i] = logs
        state = jnp.exp(log_i) * state + STI[i, pl.ds(0, WIDE), :].astype(F32)
        return state, logs + log_i

    row_state, row_logs = lax.fori_loop(
        0, 8, chain, (jnp.zeros((WIDE, WIDE), F32), jnp.zeros((1, WIDE), F32))
    )
    RT[pl.ds(0, WIDE), :] = row_state.astype(BF)
    RT[pl.ds(WIDE, 16), :] = split3(row_logs)
    RTI[y] = RT[...]
    f2 = [
        put(S_F2 + d - 1, RT, RTI.at[y], at(turn(y, d), z, c)) for d in (1, 2, 3)
    ]
    for copy in f2:
        copy.wait_recv()
    carried = jnp.zeros((WIDE, WIDE), F32)
    for yy in range(3):
        grown = jnp.exp(join3(RTI[yy, pl.ds(WIDE, 16), :])) * carried
        grown = grown + RTI[yy, pl.ds(0, WIDE), :].astype(F32)
        carried = jnp.where(yy < y, grown, carried)

    def enter(i, _):
        EN[i] = (LL[i] + jnp.exp(EP[i]) * carried).astype(BF)
        return 0

    lax.fori_loop(0, 8, enter, 0)
    ENT[grp] = EN[grp]
    f3 = []
    for d in range(1, 8):
        p, dev = mate(d)
        f3.append(put(S_F3 + d - 1, EN.at[p], ENT.at[grp], dev))

    wyf0.wait_recv()
    wyf1.wait_recv()
    wyo0 = same(S_W + 16, WB.at[yo, z, 0], ZN)
    wyo1 = same(S_W + 17, WB.at[yo, z, 0], ZP)
    wzf0.wait_recv()
    wzf1.wait_recv()
    wzo0 = same(S_W + 18, WB.at[y, zo, 1], YN)
    wzo1 = same(S_W + 19, WB.at[y, zo, 1], YP)
    w3 = []
    for i, (copy, ref, dev) in enumerate(
        (
            (wyp0, WB.at[yp, zp, 0, 0], ZN),
            (wyp1, WB.at[yp, zn, 0, 1], ZP),
            (wzp0, WB.at[yp, zp, 1, 0], YN),
            (wzp1, WB.at[yn, zp, 1, 1], YP),
            (wyn0, WB.at[yn, zp, 0, 0], ZN),
            (wyn1, WB.at[yn, zn, 0, 1], ZP),
            (wzn0, WB.at[yp, zn, 1, 0], YN),
            (wzn1, WB.at[yn, zn, 1, 1], YP),
        )
    ):
        copy.wait_recv()
        w3.append(same(S_W + 20 + i, ref, dev))

    for copy in f3:
        copy.wait_recv()

    def attend_head(h, _):
        hs = head_cols(h)
        att = ATT[:, hs] + jnp.exp(CC[h]) * dot(q[:, hs], ENT[h])
        r = lax.rsqrt(jnp.mean(att * att, axis=-1, keepdims=True) + EPSILON)
        scaled = att * r
        ATT[:, hs] = scaled
        RN[h] = r
        MX[c, :, hs] = (scaled * gain[:, hs]).astype(BF)
        return 0

    lax.fori_loop(0, HEADS, attend_head, 0)
    mix = put(S_MIX, MX.at[c], MX.at[c], SIB)

    for i, (copy, ref, dev) in enumerate(
        (
            (wyo0, WB.at[yo, zp, 0, 0], ZN),
            (wyo1, WB.at[yo, zn, 0, 1], ZP),
            (wzo0, WB.at[yp, zo, 1, 0], YN),
            (wzo1, WB.at[yn, zo, 1, 1], YP),
        )
    ):
        copy.wait_recv()
        w3.append(same(S_W + 28 + i, ref, dev))

    def weight_term(xx):
        def tile(i, _):
            pair = lax.div(i, 2)
            n = lax.rem(i, 2)
            ms = pl.ds(pl.multiple_of(pair * 384, 384), 384)
            ns = pl.ds(pl.multiple_of(n * 512, 512), 512)
            term = dot_t0(OG[xx, pl.ds(0, ROWS), ms], MX[0, :, ns])
            term = term + dot_t0(OG[xx, pl.ds(ROWS, ROWS), ms], MX[1, :, ns])
            DW[xx, pl.ds(2 * pair, 2), :, :, :, ns] = (
                term.astype(BF).reshape(2, 2, 2, QUART, 512)
            )
            return 0

        lax.fori_loop(0, 4, tile, 0)

    def delta_term(xx, first, half):
        def tile(i, _):
            m = lax.div(i, 2)
            n = lax.rem(i, 2)
            ms = pl.ds(pl.multiple_of(half * ROWS + m * BLK, BLK), BLK)
            ns = pl.ds(pl.multiple_of(n * 512, 512), 512)
            term = dot(OG[xx, ms, :], WB[xx, :, :, :, :, ns].reshape(SPAN, 512))
            if first:
                ACC[ms, ns] = term
            else:
                ACC[ms, ns] += term
            return 0

        lax.fori_loop(0, 4, tile, 0)

    def add_to(target, *more):
        total = target.astype(F32)
        for term in more:
            total = total + term.astype(F32)
        return total.astype(BF)

    b1lo = make(S_RS + 0, DW.at[yo, :, 1, 0], R1B.at[0], YN)
    b1hi = make(S_RS + 1, DW.at[yo, :, 1, 1], R1B.at[1], YP)
    b2n = make(S_RS + 2, DW.at[yn, :, 1], R2B.at[0], YN)
    b2p = make(S_RS + 3, DW.at[yp, :, 1], R2B.at[1], YP)
    c1lo = make(S_RS + 4, DW.at[yo, z, 0, 0], R3.at[0, 0], YN)
    c1hi = make(S_RS + 5, DW.at[yo, z, 0, 1], R3.at[0, 1], YP)
    c2n = make(S_RS + 6, DW.at[yn, z, 0], R4.at[0, 0], YN)
    c2p = make(S_RS + 7, DW.at[yp, z, 0], R4.at[0, 1], YP)
    d1lo = make(S_RS + 8, DW.at[y, zo, 1, 0], R3.at[1, 0], ZN)
    d1hi = make(S_RS + 9, DW.at[y, zo, 1, 1], R3.at[1, 1], ZP)
    d2n = make(S_RS + 10, DW.at[y, zn, 1], R4.at[1, 0], ZN)
    d2p = make(S_RS + 11, DW.at[y, zp, 1], R4.at[1, 1], ZP)
    live += [b1lo, b1hi, b2n, b2p, c1lo, c1hi, c2n, c2p, d1lo, d1hi, d2n, d2p]
    a1 = {}
    a2 = {}

    def reduce_1(j, xx):
        a1[j] = (
            put(S_A1 + 2 * j, DW.at[xx, zo, 0, 0], R1.at[0, j], ZN),
            put(S_A1 + 2 * j + 1, DW.at[xx, zo, 0, 1], R1.at[1, j], ZP),
        )

        @pl.when(xx == yo)
        def _():
            b1lo.start()
            b1hi.start()

    def reduce_2(j, xx):
        a1[j][0].wait_recv()
        DW[xx, zn, 0, 0] = add_to(DW[xx, zn, 0, 0], R1[0, j])
        to_n = put(S_A2 + 2 * j, DW.at[xx, zn, 0], R2.at[0, j], ZN)
        a1[j][1].wait_recv()
        DW[xx, zp, 0, 1] = add_to(DW[xx, zp, 0, 1], R1[1, j])
        to_p = put(S_A2 + 2 * j + 1, DW.at[xx, zp, 0], R2.at[1, j], ZP)
        a2[j] = (to_n, to_p)

        @pl.when(xx == yn)
        def _():
            b1lo.wait_recv()
            for i in range(4):
                DW[yn, i, 1, 0] = add_to(DW[yn, i, 1, 0], R1B[0, i])
            b2n.start()

        @pl.when(xx == yp)
        def _():
            b1hi.wait_recv()
            for i in range(4):
                DW[yp, i, 1, 1] = add_to(DW[yp, i, 1, 1], R1B[1, i])
            b2p.start()

    def reduce_3(j, xx):
        a2[j][0].wait_recv()
        a2[j][1].wait_recv()
        DW[xx, z, 0] = add_to(DW[xx, z, 0], R2[0, j], R2[1, j])

        @pl.when(xx == yo)
        def _():
            c1lo.start()
            c1hi.start()

        @pl.when(xx == y)
        def _():
            b2n.wait_recv()
            b2p.wait_recv()
            for i in range(4):
                DW[y, i, 1] = add_to(DW[y, i, 1], R2B[0, i], R2B[1, i])
            d1lo.start()
            d1hi.start()

    def reduce_4(j, xx):
        @pl.when(xx == yn)
        def _():
            c1lo.wait_recv()
            DW[yn, z, 0, 0] = add_to(DW[yn, z, 0, 0], R3[0, 0])
            c2n.start()

        @pl.when(xx == yp)
        def _():
            c1hi.wait_recv()
            DW[yp, z, 0, 1] = add_to(DW[yp, z, 0, 1], R3[0, 1])
            c2p.start()

        @pl.when(xx == y)
        def _():
            d1lo.wait_recv()
            DW[y, zn, 1, 0] = add_to(DW[y, zn, 1, 0], R3[1, 0])
            d2n.start()
            d1hi.wait_recv()
            DW[y, zp, 1, 1] = add_to(DW[y, zp, 1, 1], R3[1, 1])
            d2p.start()

    mix.wait_recv()
    weight_term(x)
    reduce_1(0, x)

    xr0.wait_recv()
    xr2 = put(S_X + 4, OG.at[xp, own_rows], OG.at[xp, own_rows], XN)
    xl0.wait_recv()
    xl2 = put(S_X + 5, OG.at[xn, sib_rows], OG.at[xn, sib_rows], XP)
    reduce_2(0, x)

    for copy in w3:
        copy.wait_recv()
    delta_term(x, True, o)
    delta_term(x, True, c)
    reduce_3(0, x)
    xr1.wait_recv()
    xl1.wait_recv()
    weight_term(xp)
    reduce_1(1, xp)
    delta_term(xp, False, o)
    delta_term(xp, False, c)
    reduce_4(0, x)
    weight_term(xn)
    reduce_1(2, xn)
    reduce_2(1, xp)
    delta_term(xn, False, o)
    delta_term(xn, False, c)
    reduce_2(2, xn)
    reduce_3(1, xp)
    xr2.wait_recv()
    xl2.wait_recv()

    ods = []
    for m in range(2):

        def last_tile(n, _):
            ms = pl.ds(pl.multiple_of(o * ROWS + m * BLK, BLK), BLK)
            ns = pl.ds(pl.multiple_of(n * 512, 512), 512)
            term = dot(OG[xo, ms, :], WB[xo, :, :, :, :, ns].reshape(SPAN, 512))
            XO[pl.ds(m * BLK, BLK), ns] = (ACC[ms, ns] + term).astype(BF)
            return 0

        lax.fori_loop(0, 2, last_tile, 0)
        part = pl.ds(m * BLK, BLK)
        ods.append(put(S_OD + m, XO.at[part], XI.at[part], SIB))
    delta_term(xo, False, c)
    weight_term(xo)
    reduce_1(3, xo)
    for copy in ods:
        copy.wait_recv()

    def norm_back_head(h):
        hs = head_cols(h)
        delta = ACC[own_rows, hs] + XI[:, hs].astype(F32)
        scaled = ATT[:, hs]
        gg = delta * gain[:, hs]
        da = RN[h] * (gg - scaled * jnp.mean(gg * scaled, axis=-1, keepdims=True))
        da = da.astype(BF)
        DA[:, hs] = da
        qd = (q[:, hs].astype(F32) * jnp.exp(CC[h])).astype(BF)
        GS[h] = dot_t0(qd, da).astype(BF)

    def first_back(d):
        p, dev = mate(d)
        return make(S_B1 + d - 1, GS.at[p], GSI.at[grp], dev)

    def norm_back_step(d, _):
        norm_back_head(lax.rem(grp + d, 8))
        first_back(d).start()
        return 0

    lax.fori_loop(1, 8, norm_back_step, 0)
    norm_back_head(grp)
    GSI[grp] = GS[grp]
    b1 = [first_back(d) for d in range(1, 8)]
    live += b1

    reduce_2(3, xo)
    reduce_3(2, xn)
    reduce_4(1, xp)
    for copy in b1:
        copy.wait_recv()

    def chain_back(n, carry):
        i = 7 - n
        state, logs = carry
        log_i = join3(STI[i, pl.ds(WIDE, 16), :])
        LL[i] = state
        EP[i] = logs
        state = jnp.exp(log_i) * state + GSI[i].astype(F32)
        return state, logs + log_i

    row_back, _ = lax.fori_loop(
        0, 8, chain_back, (jnp.zeros((WIDE, WIDE), F32), jnp.zeros((1, WIDE), F32))
    )
    GR[...] = row_back.astype(BF)
    GRI[y] = GR[...]
    b2 = [
        put(S_B2 + d - 1, GR, GRI.at[y], at(turn(y, d), z, c)) for d in (1, 2, 3)
    ]

    def local_back_head(h, _):
        hs = head_cols(h)
        dk_blk = [None, None]
        dv_blk = [None, None]
        for tb in range(2):
            da = DA[blk(tb), hs]
            out = jnp.exp(CC[h, blk(tb), :]) * dot_t1(da, ENT[h])
            for sb in range(tb + 1):
                dp = (dot_t1(da, v[blk(sb), hs]) * decays(h, tb, sb)).astype(BF)
                out = out + dot(dp, k[blk(sb), hs])
                k_term = dot_t0(dp, q[blk(tb), hs])
                v_term = dot_t0(PB[h, blk(tb), blk(sb)], da)
                dk_blk[sb] = k_term if dk_blk[sb] is None else dk_blk[sb] + k_term
                dv_blk[sb] = v_term if dv_blk[sb] is None else dv_blk[sb] + v_term
            dq[blk(tb), hs] = out.astype(BF)
        for sb in range(2):
            ACC[blk(sb), hs] = dk_blk[sb]
            ACC[blk(2 + sb), hs] = dv_blk[sb]
        return 0

    lax.fori_loop(0, 4, local_back_head, 0)

    for copy in b2:
        copy.wait_recv()
    carried_back = jnp.zeros((WIDE, WIDE), F32)
    for yy in (3, 2, 1):
        grown = jnp.exp(join3(RTI[yy, pl.ds(WIDE, 16), :])) * carried_back
        grown = grown + GRI[yy].astype(F32)
        carried_back = jnp.where(yy > y, grown, carried_back)

    def leave(i, _):
        GO[i] = (LL[i] + jnp.exp(EP[i]) * carried_back).astype(BF)
        return 0

    lax.fori_loop(0, 8, leave, 0)
    GG[grp] = GO[grp]
    b3 = []
    for d in range(1, 8):
        p, dev = mate(d)
        b3.append(put(S_B3 + d - 1, GO.at[p], GG.at[grp], dev))

    lax.fori_loop(4, 8, local_back_head, 0)

    reduce_3(3, xo)
    reduce_4(2, xn)

    for copy in b3:
        copy.wait_recv()

    def last_head(h, _):
        hs = head_cols(h)
        total = CR[h, :, pl.ds(ROWS - WIDE, WIDE)][:, WIDE - 1 : WIDE]
        tail = jnp.exp(total - CC[h])
        dk[:, hs] = (ACC[pl.ds(0, ROWS), hs] + tail * dot_t1(v[:, hs], GG[h])).astype(BF)
        dv[:, hs] = (ACC[pl.ds(ROWS, ROWS), hs] + tail * dot(k[:, hs], GG[h])).astype(BF)
        return 0

    lax.fori_loop(0, 4, last_head, 0)

    reduce_4(3, xo)
    lax.fori_loop(4, 8, last_head, 0)

    for half, (from_p, from_n) in enumerate(((c2n, c2p), (d2n, d2p))):
        from_p.wait_recv()
        from_n.wait_recv()
        for i in range(2):
            dw[pl.ds(half * HALF + i * QUART, QUART), :] = (
                DW[y, z, half, i].astype(F32)
                + R4[half, 0, i].astype(F32)
                + R4[half, 1, i].astype(F32)
            ) * SCALE

    for copy in live:
        copy.wait_send()


def body(query_rows, key_rows, value_rows, log_decay, norm_gain, out_weight, out_grad):
    vm = pltpu.VMEM
    scratch = [
        vm((4, 2 * ROWS, SPAN), BF),
        vm((ROWS, SPAN), BF),
        vm((4, 4, 2, 2, QUART, COLS), BF),
        vm((2 * ROWS, COLS), F32),
        vm((ROWS, COLS), BF),
        vm((ROWS, COLS), BF),
        vm((2, ROWS, COLS), BF),
        vm((4, 4, 2, 2, QUART, COLS), BF),
        vm((2, 4, QUART, COLS), BF),
        vm((2, 4, 2, QUART, COLS), BF),
        vm((2, 2, QUART, COLS), BF),
        vm((2, 2, 2, QUART, COLS), BF),
        vm((2, 4, QUART, COLS), BF),
        vm((2, 4, 2, QUART, COLS), BF),
        vm((HEADS, ROWS, ROWS), BF),
        vm((ROWS, COLS), F32),
        vm((ROWS, COLS), BF),
        vm((HEADS, ROWS, 1), F32),
        vm((HEADS, ROWS, 1), F32),
        vm((HEADS, 1, ROWS), F32),
        vm((8, WIDE + 16, WIDE), BF),
        vm((8, WIDE + 16, WIDE), BF),
        vm((WIDE + 16, WIDE), BF),
        vm((4, WIDE + 16, WIDE), BF),
        vm((8, WIDE, WIDE), BF),
        vm((8, WIDE, WIDE), BF),
        vm((8, WIDE, WIDE), F32),
        vm((8, 1, WIDE), F32),
        vm((8, WIDE, WIDE), BF),
        vm((8, WIDE, WIDE), BF),
        vm((WIDE, WIDE), BF),
        vm((4, WIDE, WIDE), BF),
        vm((8, WIDE, WIDE), BF),
        vm((8, WIDE, WIDE), BF),
        pltpu.SemaphoreType.DMA((S_ALL,)),
        pltpu.SemaphoreType.DMA((S_ALL,)),
    ]
    spec = pl.BlockSpec(memory_space=pltpu.VMEM)
    return pl.pallas_call(
        kernel,
        out_shape=(
            jax.ShapeDtypeStruct((ROWS, COLS), BF),
            jax.ShapeDtypeStruct((ROWS, COLS), BF),
            jax.ShapeDtypeStruct((ROWS, COLS), BF),
            jax.ShapeDtypeStruct((UNIT, COLS), F32),
        ),
        in_specs=[spec] * 7,
        out_specs=(spec,) * 4,
        scratch_shapes=scratch,
        compiler_params=pltpu.CompilerParams(
            collective_id=0, has_side_effects=True, vmem_limit_bytes=62 * 2**20
        ),
    )(
        query_rows,
        key_rows,
        value_rows,
        log_decay,
        norm_gain.reshape(1, COLS),
        out_weight,
        out_grad,
    )


def solution(mesh):
    both = P("seq", "head")
    return jax.shard_map(
        body,
        mesh=mesh,
        in_specs=(both, both, both, P("head", "seq"), P("head"), both, both),
        out_specs=(both, both, both, both),
        check_vma=False,
    )
```

```python
import jax
import jax.numpy as jnp
from jax import lax
from jax.experimental import pallas as pl
from jax.experimental.pallas import tpu as pltpu
from jax.sharding import PartitionSpec as P

MESH = pl.DeviceIdType.MESH
BF = jnp.bfloat16
F32 = jnp.float32
HIGH = lax.Precision.HIGHEST
EPSILON = 1e-06

ROWS = 512
HEADS = 8
WIDE = 128
COLS = 1024
UNIT = 192
HALF = 96
QUART = 48
SPAN = 768
BLK = 256
SCALE = 1.0 / 128.0

S_SIB = 0
S_X = 1
S_MIX = 7
S_OD = 8
S_W = 10
S_A1 = 42
S_A2 = 50
S_RS = 58
S_E = 70
S_F1 = 78
S_F2 = 85
S_F3 = 88
S_B1 = 95
S_B2 = 102
S_B3 = 105
S_ALL = 112


def dot(a, b):
    return lax.dot_general(a, b, (((1,), (0,)), ((), ())), preferred_element_type=F32)


def dot_t0(a, b):
    return lax.dot_general(a, b, (((0,), (0,)), ((), ())), preferred_element_type=F32)


def dot_t1(a, b):
    return lax.dot_general(a, b, (((1,), (1,)), ((), ())), preferred_element_type=F32)


def kernel(
    q, k, v, ld, gain, w, g,
    dq, dk, dv, dw,
    OG, OGS, WB, ACC, XO, XI, MX, DW, R1, R2, R3, R4, R1B, R2B, E1, E2, E3, E4,
    PB, ATT, DA, CC, RN, CR,
    ST, STI, RT, RTI, EN, ENT, LL, EP,
    GS, GSI, GR, GRI, GO, GG,
    ss, rs,
):
    me = lax.axis_index("seq")
    x = lax.axis_index("head")
    y = lax.div(me, 8)
    grp = lax.rem(me, 8)
    z = lax.div(grp, 2)
    c = lax.rem(me, 2)
    o = 1 - c

    def turn(a, d):
        return lax.rem(a + d, 4)

    yn, yo, yp = turn(y, 1), turn(y, 2), turn(y, 3)
    zn, zo, zp = turn(z, 1), turn(z, 2), turn(z, 3)
    xn, xo, xp = turn(x, 1), turn(x, 2), turn(x, 3)

    def at(yy, zz, cc):
        return ((yy * 4 + zz) * 2 + cc, x)

    YN, YP, ZN, ZP = at(yn, z, c), at(yp, z, c), at(y, zn, c), at(y, zp, c)
    XN, XP = (me, xn), (me, xp)
    SIB = at(y, z, o)

    def mate(d):
        p = lax.rem(grp + d, 8)
        return p, (y * 8 + p, x)

    live = []

    def make(i, src, dst, dev):
        return pltpu.make_async_remote_copy(
            src_ref=src,
            dst_ref=dst,
            send_sem=ss.at[i],
            recv_sem=rs.at[i],
            device_id=dev,
            device_id_type=MESH,
        )

    def put(i, src, dst, dev):
        copy = make(i, src, dst, dev)
        copy.start()
        live.append(copy)
        return copy

    def same(i, ref, dev):
        return put(i, ref, ref, dev)

    barrier = pltpu.get_barrier_semaphore()
    partners = [mate(d)[1] for d in range(1, 8)]
    partners += [at(turn(y, d), z, c) for d in (1, 2, 3)]
    partners += [XN, XP]
    for dev in partners:
        pl.semaphore_signal(barrier, inc=1, device_id=dev, device_id_type=MESH)
    pl.semaphore_wait(barrier, len(partners))

    own_rows = pl.ds(pl.multiple_of(c * ROWS, ROWS), ROWS)
    sib_rows = pl.ds(pl.multiple_of(o * ROWS, ROWS), ROWS)

    half = (pl.ds(0, HALF), pl.ds(HALF, HALF))
    quart = tuple(tuple(pl.ds(a * HALF + b * QUART, QUART) for b in range(2)) for a in range(2))

    WB[y, z] = w[...]
    wy0 = same(S_W + 0, WB.at[y, z], YN)
    wy1 = same(S_W + 1, WB.at[y, z], YP)
    wz0 = same(S_W + 2, WB.at[y, z], ZN)
    wz1 = same(S_W + 3, WB.at[y, z], ZP)

    for part in range(4):
        r = pl.ds(part * 128, 128)
        rows = g[r, :]
        even = jnp.concatenate(
            [rows[:, (2 * i) * UNIT : (2 * i + 1) * UNIT] for i in range(4)], axis=1
        )
        odd = jnp.concatenate(
            [rows[:, (2 * i + 1) * UNIT : (2 * i + 2) * UNIT] for i in range(4)], axis=1
        )
        mine = jnp.where(c == 0, even, odd)
        other = jnp.where(c == 0, odd, even)
        OG[x, pl.ds(pl.multiple_of(c * ROWS + part * 128, 128), 128), :] = mine
        OGS[r, :] = other
    sib = put(S_SIB, OGS, OG.at[x, own_rows], SIB)
    xr0 = put(S_X + 0, OG.at[x, own_rows], OG.at[x, own_rows], XN)
    xl1 = put(S_X + 3, OG.at[x, own_rows], OG.at[x, own_rows], XP)

    row_i = lax.broadcasted_iota(jnp.int32, (ROWS, ROWS), 0)
    col_i = lax.broadcasted_iota(jnp.int32, (ROWS, ROWS), 1)
    upper = (row_i <= col_i).astype(F32)
    lower = (row_i >= col_i).astype(F32)
    by_rows = lax.dot_general(
        ld[...], upper, (((1,), (0,)), ((), ())), precision=HIGH, preferred_element_type=F32
    )
    by_cols = lax.dot_general(
        lower, ld[...], (((1,), (1,)), ((), ())), precision=HIGH, preferred_element_type=F32
    )
    for h in range(HEADS):
        CR[h] = by_rows[h : h + 1, :]
        CC[h] = jnp.broadcast_to(by_cols[:, h : h + 1], (ROWS, WIDE))

    sib.wait_recv()
    xl0 = put(S_X + 2, OG.at[x, sib_rows], OG.at[x, sib_rows], XP)
    xr1 = put(S_X + 1, OG.at[x, sib_rows], OG.at[x, sib_rows], XN)

    def head_cols(h):
        return pl.ds(pl.multiple_of(h * WIDE, WIDE), WIDE)

    def decays(h, tb, sb):
        cc = CC[h, pl.ds(tb * BLK, BLK), :]
        cr = CR[h, :, pl.ds(sb * BLK, BLK)]
        grown = jnp.exp(jnp.concatenate([cc, cc], axis=1) - cr)
        if tb == sb:
            t = lax.broadcasted_iota(jnp.int32, (BLK, BLK), 0)
            s = lax.broadcasted_iota(jnp.int32, (BLK, BLK), 1)
            grown = jnp.where(t >= s, grown, 0.0)
        return grown

    def blk(b):
        return pl.ds(b * BLK, BLK)

    row16 = lax.broadcasted_iota(jnp.int32, (16, WIDE), 0)

    def split3(row):
        hi = row.astype(BF).astype(F32)
        mid = (row - hi).astype(BF).astype(F32)
        lo = (row - hi - mid).astype(BF).astype(F32)
        full = jnp.where(
            row16 == 0, hi, jnp.where(row16 == 1, mid, jnp.where(row16 == 2, lo, 0.0))
        )
        return full.astype(BF)

    def join3(block):
        return jnp.sum(block.astype(F32), axis=0, keepdims=True)

    def forward_head(h):
        hs = head_cols(h)
        for tb in range(2):
            out = jnp.zeros((BLK, WIDE), F32)
            for sb in range(tb + 1):
                scores = dot_t1(q[blk(tb), hs], k[blk(sb), hs])
                p = (scores * decays(h, tb, sb)).astype(BF)
                PB[h, blk(tb), blk(sb)] = p
                out = out + dot(p, v[blk(sb), hs])
            ATT[blk(tb), hs] = out
        total = CR[h, :, pl.ds(ROWS - WIDE, WIDE)][:, WIDE - 1 : WIDE]
        kd = (k[:, hs].astype(F32) * jnp.exp(total - CC[h])).astype(BF)
        ST[h, pl.ds(0, WIDE), :] = dot_t0(kd, v[:, hs]).astype(BF)
        ST[h, pl.ds(WIDE, 16), :] = split3(jnp.broadcast_to(total, (1, WIDE)))

    def first(d):
        p, dev = mate(d)
        return make(S_F1 + d - 1, ST.at[p], STI.at[grp], dev)

    def forward_step(d, _):
        forward_head(lax.rem(grp + d, 8))
        first(d).start()
        return 0

    lax.fori_loop(1, 8, forward_step, 0)
    forward_head(grp)
    STI[grp] = ST[grp]
    f1 = [first(d) for d in range(1, 8)]
    live += f1

    wy0.wait_recv()
    wyf0 = same(S_W + 4, WB.at[yp, z, half[0]], YN)
    wyp0 = same(S_W + 5, WB.at[yp, z, half[0]], ZN)
    wyp1 = same(S_W + 6, WB.at[yp, z, half[0]], ZP)
    wy1.wait_recv()
    wyf1 = same(S_W + 7, WB.at[yn, z, half[1]], YP)
    wyn0 = same(S_W + 8, WB.at[yn, z, half[0]], ZN)
    wyn1 = same(S_W + 9, WB.at[yn, z, half[0]], ZP)
    wz0.wait_recv()
    wzf0 = same(S_W + 10, WB.at[y, zp, half[0]], ZN)
    wzp0 = same(S_W + 11, WB.at[y, zp, half[1]], YN)
    wzp1 = same(S_W + 12, WB.at[y, zp, half[1]], YP)
    wz1.wait_recv()
    wzf1 = same(S_W + 13, WB.at[y, zn, half[1]], ZP)
    wzn0 = same(S_W + 14, WB.at[y, zn, half[1]], YN)
    wzn1 = same(S_W + 15, WB.at[y, zn, half[1]], YP)

    for copy in f1:
        copy.wait_recv()

    def chain(i, carry):
        state, logs = carry
        log_i = join3(STI[i, pl.ds(WIDE, 16), :])
        LL[i] = state
        EP[i] = logs
        state = jnp.exp(log_i) * state + STI[i, pl.ds(0, WIDE), :].astype(F32)
        return state, logs + log_i

    row_state, row_logs = lax.fori_loop(
        0, 8, chain, (jnp.zeros((WIDE, WIDE), F32), jnp.zeros((1, WIDE), F32))
    )
    RT[pl.ds(0, WIDE), :] = row_state.astype(BF)
    RT[pl.ds(WIDE, 16), :] = split3(row_logs)
    RTI[y] = RT[...]
    f2 = [
        put(S_F2 + d - 1, RT, RTI.at[y], at(turn(y, d), z, c)) for d in (1, 2, 3)
    ]
    for copy in f2:
        copy.wait_recv()
    carried = jnp.zeros((WIDE, WIDE), F32)
    for yy in range(3):
        grown = jnp.exp(join3(RTI[yy, pl.ds(WIDE, 16), :])) * carried
        grown = grown + RTI[yy, pl.ds(0, WIDE), :].astype(F32)
        carried = jnp.where(yy < y, grown, carried)

    def enter(i, _):
        EN[i] = (LL[i] + jnp.exp(EP[i]) * carried).astype(BF)
        return 0

    lax.fori_loop(0, 8, enter, 0)
    ENT[grp] = EN[grp]
    f3 = []
    for d in range(1, 8):
        p, dev = mate(d)
        f3.append(put(S_F3 + d - 1, EN.at[p], ENT.at[grp], dev))

    wyf0.wait_recv()
    wyf1.wait_recv()
    wyo0 = same(S_W + 16, WB.at[yo, z, half[0]], ZN)
    wyo1 = same(S_W + 17, WB.at[yo, z, half[0]], ZP)
    wzf0.wait_recv()
    wzf1.wait_recv()
    wzo0 = same(S_W + 18, WB.at[y, zo, half[1]], YN)
    wzo1 = same(S_W + 19, WB.at[y, zo, half[1]], YP)
    w3 = []
    for i, (copy, ref, dev) in enumerate(
        (
            (wyp0, WB.at[yp, zp, quart[0][0]], ZN),
            (wyp1, WB.at[yp, zn, quart[0][1]], ZP),
            (wzp0, WB.at[yp, zp, quart[1][0]], YN),
            (wzp1, WB.at[yn, zp, quart[1][1]], YP),
            (wyn0, WB.at[yn, zp, quart[0][0]], ZN),
            (wyn1, WB.at[yn, zn, quart[0][1]], ZP),
            (wzn0, WB.at[yp, zn, quart[1][0]], YN),
            (wzn1, WB.at[yn, zn, quart[1][1]], YP),
        )
    ):
        copy.wait_recv()
        w3.append(same(S_W + 20 + i, ref, dev))

    for copy in f3:
        copy.wait_recv()

    mean_of = jnp.full((WIDE, WIDE), 1.0 / WIDE, BF)

    def attend_head(h, _):
        hs = head_cols(h)
        att = ATT[:, hs] + jnp.exp(CC[h]) * dot(q[:, hs], ENT[h])
        square = att * att
        high = square.astype(BF)
        low = (square - high.astype(F32)).astype(BF)
        r = lax.rsqrt(dot(high, mean_of) + dot(low, mean_of) + EPSILON)
        scaled = att * r
        ATT[:, hs] = scaled
        RN[h] = r
        MX[c, :, hs] = (scaled * gain[:, hs]).astype(BF)
        return 0

    lax.fori_loop(0, HEADS, attend_head, 0)
    mix = put(S_MIX, MX.at[c], MX.at[c], SIB)

    for i, (copy, ref, dev) in enumerate(
        (
            (wyo0, WB.at[yo, zp, quart[0][0]], ZN),
            (wyo1, WB.at[yo, zn, quart[0][1]], ZP),
            (wzo0, WB.at[yp, zo, quart[1][0]], YN),
            (wzo1, WB.at[yn, zo, quart[1][1]], YP),
        )
    ):
        copy.wait_recv()
        w3.append(same(S_W + 28 + i, ref, dev))

    def weight_term(xx):
        def tile(i, _):
            pair = lax.div(i, 2)
            n = lax.rem(i, 2)
            ms = pl.ds(pl.multiple_of(pair * 384, 384), 384)
            ns = pl.ds(pl.multiple_of(n * 512, 512), 512)
            term = dot_t0(OG[xx, pl.ds(0, ROWS), ms], MX[0, :, ns])
            term = term + dot_t0(OG[xx, pl.ds(ROWS, ROWS), ms], MX[1, :, ns])
            DW[xx, pl.ds(2 * pair, 2), :, ns] = term.reshape(2, UNIT, 512).astype(BF)
            return 0

        lax.fori_loop(0, 4, tile, 0)

    def delta_term(xx, first, half):
        def tile(i, _):
            m = lax.div(i, 2)
            n = lax.rem(i, 2)
            ms = pl.ds(pl.multiple_of(half * ROWS + m * BLK, BLK), BLK)
            ns = pl.ds(pl.multiple_of(n * 512, 512), 512)
            term = dot(OG[xx, ms, :], WB[xx, :, :, ns].reshape(SPAN, 512))
            if first:
                ACC[ms, ns] = term
            else:
                ACC[ms, ns] += term
            return 0

        lax.fori_loop(0, 4, tile, 0)

    def add_to(target, *more):
        total = target.astype(F32)
        for term in more:
            total = total + term.astype(F32)
        return total.astype(BF)

    early = ((0, x), (1, xp), (2, xn))
    b1lo = make(S_RS + 0, DW.at[yo, :, quart[1][0]], R1B.at[0], YN)
    b1hi = make(S_RS + 1, DW.at[yo, :, quart[1][1]], R1B.at[1], YP)
    b2n = make(S_RS + 2, DW.at[yn, :, half[1]], R2B.at[0], YN)
    b2p = make(S_RS + 3, DW.at[yp, :, half[1]], R2B.at[1], YP)
    c1lo = make(S_RS + 4, DW.at[yo, z, quart[0][0]], R3.at[0, 0], YN)
    c1hi = make(S_RS + 5, DW.at[yo, z, quart[0][1]], R3.at[0, 1], YP)
    c2n = make(S_RS + 6, DW.at[yn, z, half[0]], R4.at[0, 0], YN)
    c2p = make(S_RS + 7, DW.at[yp, z, half[0]], R4.at[0, 1], YP)
    d1lo = make(S_RS + 8, DW.at[y, zo, quart[1][0]], R3.at[1, 0], ZN)
    d1hi = make(S_RS + 9, DW.at[y, zo, quart[1][1]], R3.at[1, 1], ZP)
    d2n = make(S_RS + 10, DW.at[y, zn, half[1]], R4.at[1, 0], ZN)
    d2p = make(S_RS + 11, DW.at[y, zp, half[1]], R4.at[1, 1], ZP)
    e1lo = make(S_E + 0, DW.at[xo, zo, half[0]], E1.at[0], ZN)
    e1hi = make(S_E + 1, DW.at[xo, zo, half[1]], E1.at[1], ZP)
    e2n = make(S_E + 2, DW.at[xo, zn], E2.at[0], ZN)
    e2p = make(S_E + 3, DW.at[xo, zp], E2.at[1], ZP)
    f1lo = make(S_E + 4, DW.at[xo, z, half[0]], E3.at[0], YN)
    f1hi = make(S_E + 5, DW.at[xo, z, half[1]], E3.at[1], YP)
    f2n = make(S_E + 6, DW.at[xo, z], E4.at[0], YN)
    f2p = make(S_E + 7, DW.at[xo, z], E4.at[1], YP)
    live += [e1lo, e1hi, e2n, e2p]
    a1 = {}
    a2 = {}

    def first_hop(j, xx):
        a1[j] = (
            put(S_A1 + 2 * j, DW.at[xx, zo, quart[0][0]], R1.at[0, j], ZN),
            put(S_A1 + 2 * j + 1, DW.at[xx, zo, quart[0][1]], R1.at[1, j], ZP),
        )

    def first_hop_y():
        @pl.when(yo != xo)
        def _():
            b1lo.start()
            b1hi.start()

    def second_hop():
        for j, xx in early:
            a1[j][0].wait_recv()
            DW[xx, zn, quart[0][0]] = add_to(DW[xx, zn, quart[0][0]], R1[0, j])
            to_n = put(S_A2 + 2 * j, DW.at[xx, zn, half[0]], R2.at[0, j], ZN)
            a1[j][1].wait_recv()
            DW[xx, zp, quart[0][1]] = add_to(DW[xx, zp, quart[0][1]], R1[1, j])
            to_p = put(S_A2 + 2 * j + 1, DW.at[xx, zp, half[0]], R2.at[1, j], ZP)
            a2[j] = (to_n, to_p)

        @pl.when(yn != xo)
        def _():
            b1lo.wait_recv()
            for i in range(4):
                DW[yn, i, quart[1][0]] = add_to(DW[yn, i, quart[1][0]], R1B[0, i])
            b2n.start()

        @pl.when(yp != xo)
        def _():
            b1hi.wait_recv()
            for i in range(4):
                DW[yp, i, quart[1][1]] = add_to(DW[yp, i, quart[1][1]], R1B[1, i])
            b2p.start()

    def third_hop():
        for j, xx in early:
            a2[j][0].wait_recv()
            a2[j][1].wait_recv()
            DW[xx, z, half[0]] = add_to(DW[xx, z, half[0]], R2[0, j], R2[1, j])

        @pl.when(yo != xo)
        def _():
            c1lo.start()
            c1hi.start()

        @pl.when(y != xo)
        def _():
            b2n.wait_recv()
            b2p.wait_recv()
            for i in range(4):
                DW[y, i, half[1]] = add_to(DW[y, i, half[1]], R2B[0, i], R2B[1, i])
            d1lo.start()
            d1hi.start()

    def fourth_hop():
        @pl.when(yn != xo)
        def _():
            c1lo.wait_recv()
            DW[yn, z, quart[0][0]] = add_to(DW[yn, z, quart[0][0]], R3[0, 0])
            c2n.start()

        @pl.when(yp != xo)
        def _():
            c1hi.wait_recv()
            DW[yp, z, quart[0][1]] = add_to(DW[yp, z, quart[0][1]], R3[0, 1])
            c2p.start()

        @pl.when(y != xo)
        def _():
            d1lo.wait_recv()
            DW[y, zn, quart[1][0]] = add_to(DW[y, zn, quart[1][0]], R3[1, 0])
            d2n.start()
            d1hi.wait_recv()
            DW[y, zp, quart[1][1]] = add_to(DW[y, zp, quart[1][1]], R3[1, 1])
            d2p.start()

    def late_second_hop():
        e1lo.wait_recv()
        DW[xo, zn, half[0]] = add_to(DW[xo, zn, half[0]], E1[0])
        e2n.start()
        e1hi.wait_recv()
        DW[xo, zp, half[1]] = add_to(DW[xo, zp, half[1]], E1[1])
        e2p.start()

    def late_third_hop():
        e2n.wait_recv()
        e2p.wait_recv()
        for i in range(2):
            DW[xo, z, half[i]] = add_to(DW[xo, z, half[i]], E2[0, half[i]], E2[1, half[i]])

        @pl.when(yo == xo)
        def _():
            f1lo.start()
            f1hi.start()

    def late_fourth_hop():
        @pl.when(yn == xo)
        def _():
            f1lo.wait_recv()
            DW[xo, z, half[0]] = add_to(DW[xo, z, half[0]], E3[0])
            f2n.start()

        @pl.when(yp == xo)
        def _():
            f1hi.wait_recv()
            DW[xo, z, half[1]] = add_to(DW[xo, z, half[1]], E3[1])
            f2p.start()

    mix.wait_recv()
    weight_term(x)
    first_hop(0, x)

    xr0.wait_recv()
    xr2 = put(S_X + 4, OG.at[xp, own_rows], OG.at[xp, own_rows], XN)
    xl0.wait_recv()
    xl2 = put(S_X + 5, OG.at[xn, sib_rows], OG.at[xn, sib_rows], XP)
    xr1.wait_recv()
    weight_term(xp)
    first_hop(1, xp)
    xl1.wait_recv()
    weight_term(xn)
    first_hop(2, xn)
    first_hop_y()

    for copy in w3:
        copy.wait_recv()
    delta_term(x, True, o)
    delta_term(x, True, c)
    delta_term(xp, False, o)
    delta_term(xp, False, c)
    second_hop()
    delta_term(xn, False, o)
    delta_term(xn, False, c)
    xr2.wait_recv()
    xl2.wait_recv()

    ods = []
    for m in range(2):

        def last_tile(n, _):
            ms = pl.ds(pl.multiple_of(o * ROWS + m * BLK, BLK), BLK)
            ns = pl.ds(pl.multiple_of(n * 512, 512), 512)
            term = dot(OG[xo, ms, :], WB[xo, :, :, ns].reshape(SPAN, 512))
            XO[pl.ds(m * BLK, BLK), ns] = (ACC[ms, ns] + term).astype(BF)
            return 0

        lax.fori_loop(0, 2, last_tile, 0)
        part = pl.ds(m * BLK, BLK)
        ods.append(put(S_OD + m, XO.at[part], XI.at[part], SIB))
    delta_term(xo, False, c)
    weight_term(xo)
    e1lo.start()
    e1hi.start()
    for copy in ods:
        copy.wait_recv()

    def norm_back_head(h):
        hs = head_cols(h)
        delta = ACC[own_rows, hs] + XI[:, hs].astype(F32)
        scaled = ATT[:, hs]
        gg = delta * gain[:, hs]
        da = RN[h] * (gg - scaled * dot((gg * scaled).astype(BF), mean_of))
        da = da.astype(BF)
        DA[:, hs] = da
        qd = (q[:, hs].astype(F32) * jnp.exp(CC[h])).astype(BF)
        GS[h] = dot_t0(qd, da).astype(BF)

    def first_back(d):
        p, dev = mate(d)
        return make(S_B1 + d - 1, GS.at[p], GSI.at[grp], dev)

    def norm_back_step(d, _):
        norm_back_head(lax.rem(grp + d, 8))
        first_back(d).start()
        return 0

    lax.fori_loop(1, 8, norm_back_step, 0)
    norm_back_head(grp)
    GSI[grp] = GS[grp]
    b1 = [first_back(d) for d in range(1, 8)]
    live += b1

    third_hop()
    for copy in b1:
        copy.wait_recv()

    def chain_back(n, carry):
        i = 7 - n
        state, logs = carry
        log_i = join3(STI[i, pl.ds(WIDE, 16), :])
        LL[i] = state
        EP[i] = logs
        state = jnp.exp(log_i) * state + GSI[i].astype(F32)
        return state, logs + log_i

    row_back, _ = lax.fori_loop(
        0, 8, chain_back, (jnp.zeros((WIDE, WIDE), F32), jnp.zeros((1, WIDE), F32))
    )
    GR[...] = row_back.astype(BF)
    GRI[y] = GR[...]
    b2 = [
        put(S_B2 + d - 1, GR, GRI.at[y], at(turn(y, d), z, c)) for d in (1, 2, 3)
    ]

    def local_back_head(h, _):
        hs = head_cols(h)
        dk_blk = [None, None]
        dv_blk = [None, None]
        for tb in range(2):
            da = DA[blk(tb), hs]
            out = jnp.exp(CC[h, blk(tb), :]) * dot_t1(da, ENT[h])
            for sb in range(tb + 1):
                dp = (dot_t1(da, v[blk(sb), hs]) * decays(h, tb, sb)).astype(BF)
                out = out + dot(dp, k[blk(sb), hs])
                k_term = dot_t0(dp, q[blk(tb), hs])
                v_term = dot_t0(PB[h, blk(tb), blk(sb)], da)
                dk_blk[sb] = k_term if dk_blk[sb] is None else dk_blk[sb] + k_term
                dv_blk[sb] = v_term if dv_blk[sb] is None else dv_blk[sb] + v_term
            dq[blk(tb), hs] = out.astype(BF)
        for sb in range(2):
            ACC[blk(sb), hs] = dk_blk[sb]
            ACC[blk(2 + sb), hs] = dv_blk[sb]
        return 0

    late_second_hop()
    lax.fori_loop(0, 4, local_back_head, 0)

    for copy in b2:
        copy.wait_recv()
    carried_back = jnp.zeros((WIDE, WIDE), F32)
    for yy in (3, 2, 1):
        grown = jnp.exp(join3(RTI[yy, pl.ds(WIDE, 16), :])) * carried_back
        grown = grown + GRI[yy].astype(F32)
        carried_back = jnp.where(yy > y, grown, carried_back)

    def leave(i, _):
        GO[i] = (LL[i] + jnp.exp(EP[i]) * carried_back).astype(BF)
        return 0

    lax.fori_loop(0, 8, leave, 0)
    GG[grp] = GO[grp]
    b3 = []
    for d in range(1, 8):
        p, dev = mate(d)
        b3.append(put(S_B3 + d - 1, GO.at[p], GG.at[grp], dev))

    fourth_hop()
    lax.fori_loop(4, 8, local_back_head, 0)
    late_third_hop()

    def last_head(h):
        hs = head_cols(h)
        total = CR[h, :, pl.ds(ROWS - WIDE, WIDE)][:, WIDE - 1 : WIDE]
        tail = jnp.exp(total - CC[h])
        dk[:, hs] = (ACC[pl.ds(0, ROWS), hs] + tail * dot_t1(v[:, hs], GG[h])).astype(BF)
        dv[:, hs] = (ACC[pl.ds(ROWS, ROWS), hs] + tail * dot(k[:, hs], GG[h])).astype(BF)

    last_head(grp)

    def last_step(d, _):
        p = lax.rem(grp + 8 - d, 8)
        make(S_B3 + d - 1, GO.at[p], GG.at[grp], SIB).wait_recv()
        last_head(p)
        return 0

    lax.fori_loop(1, 4, last_step, 0)
    late_fourth_hop()
    lax.fori_loop(4, 8, last_step, 0)

    @pl.when(y != xo)
    def _():
        for i, (from_p, from_n) in enumerate(((c2n, c2p), (d2n, d2p))):
            from_p.wait_recv()
            from_n.wait_recv()
            dw[half[i], :] = (
                DW[y, z, half[i]].astype(F32) + R4[i, 0].astype(F32) + R4[i, 1].astype(F32)
            ) * SCALE

    @pl.when(y == xo)
    def _():
        f2n.wait_recv()
        f2p.wait_recv()
        for i in range(2):
            dw[half[i], :] = (
                DW[y, z, half[i]].astype(F32)
                + E4[0, half[i]].astype(F32)
                + E4[1, half[i]].astype(F32)
            ) * SCALE

    for place, copies in (
        (yo, (b1lo, b1hi, c1lo, c1hi)),
        (yn, (b2n, c2n)),
        (yp, (b2p, c2p)),
        (y, (d1lo, d1hi, d2n, d2p)),
    ):

        @pl.when(place != xo)
        def _():
            for copy in copies:
                copy.wait_send()

    for place, copies in ((yo, (f1lo, f1hi)), (yn, (f2n,)), (yp, (f2p,))):

        @pl.when(place == xo)
        def _():
            for copy in copies:
                copy.wait_send()

    for copy in live:
        copy.wait_send()


def hand_over(a, b, c, d, to_a, to_b, to_c, to_d, sems):
    pairs = ((a, to_a), (b, to_b), (c, to_c), (d, to_d))
    copies = [pltpu.make_async_copy(s, t, sems.at[i]) for i, (s, t) in enumerate(pairs)]
    for copy in copies:
        copy.start()
    for copy in copies:
        copy.wait()


def body(query_rows, key_rows, value_rows, log_decay, norm_gain, out_weight, out_grad):
    vm = pltpu.VMEM
    scratch = [
        vm((4, 2 * ROWS, SPAN), BF),
        vm((ROWS, SPAN), BF),
        vm((4, 4, UNIT, COLS), BF),
        vm((2 * ROWS, COLS), F32),
        vm((ROWS, COLS), BF),
        vm((ROWS, COLS), BF),
        vm((2, ROWS, COLS), BF),
        vm((4, 4, UNIT, COLS), BF),
        vm((2, 3, QUART, COLS), BF),
        vm((2, 3, HALF, COLS), BF),
        vm((2, 2, QUART, COLS), BF),
        vm((2, 2, HALF, COLS), BF),
        vm((2, 4, QUART, COLS), BF),
        vm((2, 4, HALF, COLS), BF),
        vm((2, HALF, COLS), BF),
        vm((2, UNIT, COLS), BF),
        vm((2, HALF, COLS), BF),
        vm((2, UNIT, COLS), BF),
        vm((HEADS, ROWS, ROWS), BF),
        vm((ROWS, COLS), F32),
        vm((ROWS, COLS), BF),
        vm((HEADS, ROWS, WIDE), F32),
        vm((HEADS, ROWS, WIDE), F32),
        vm((HEADS, 1, ROWS), F32),
        vm((8, WIDE + 16, WIDE), BF),
        vm((8, WIDE + 16, WIDE), BF),
        vm((WIDE + 16, WIDE), BF),
        vm((4, WIDE + 16, WIDE), BF),
        vm((8, WIDE, WIDE), BF),
        vm((8, WIDE, WIDE), BF),
        vm((8, WIDE, WIDE), F32),
        vm((8, 1, WIDE), F32),
        vm((8, WIDE, WIDE), BF),
        vm((8, WIDE, WIDE), BF),
        vm((WIDE, WIDE), BF),
        vm((4, WIDE, WIDE), BF),
        vm((8, WIDE, WIDE), BF),
        vm((8, WIDE, WIDE), BF),
        pltpu.SemaphoreType.DMA((S_ALL,)),
        pltpu.SemaphoreType.DMA((S_ALL,)),
    ]
    spec = pl.BlockSpec(memory_space=pltpu.VMEM)
    shapes = (
        jax.ShapeDtypeStruct((ROWS, COLS), BF),
        jax.ShapeDtypeStruct((ROWS, COLS), BF),
        jax.ShapeDtypeStruct((ROWS, COLS), BF),
        jax.ShapeDtypeStruct((UNIT, COLS), F32),
    )
    results = pl.pallas_call(
        kernel,
        out_shape=shapes,
        in_specs=[spec] * 7,
        out_specs=(spec,) * 4,
        scratch_shapes=scratch,
        compiler_params=pltpu.CompilerParams(
            collective_id=0, has_side_effects=True, vmem_limit_bytes=62 * 2**20
        ),
    )(
        query_rows,
        key_rows,
        value_rows,
        log_decay,
        norm_gain.reshape(1, COLS),
        out_weight,
        out_grad,
    )
    anywhere = pl.BlockSpec(memory_space=pl.ANY)
    return pl.pallas_call(
        hand_over,
        out_shape=shapes,
        in_specs=[anywhere] * 4,
        out_specs=(anywhere,) * 4,
        scratch_shapes=[pltpu.SemaphoreType.DMA((4,))],
    )(*results)


def solution(mesh):
    both = P("seq", "head")
    return jax.shard_map(
        body,
        mesh=mesh,
        in_specs=(both, both, both, P("head", "seq"), P("head"), both, both),
        out_specs=(both, both, both, both),
        check_vma=False,
    )
```

```python
import jax
import jax.numpy as jnp
from jax import lax
from jax.experimental import pallas as pl
from jax.experimental.pallas import tpu as pltpu
from jax.sharding import PartitionSpec as P

MESH = pl.DeviceIdType.MESH
BF = jnp.bfloat16
F32 = jnp.float32
HIGH = lax.Precision.HIGHEST
EPSILON = 1e-06

ROWS = 512
HEADS = 8
WIDE = 128
COLS = 1024
UNIT = 192
HALF = 96
QUART = 48
SPAN = 768
BLK = 256
SCALE = 1.0 / 128.0

S_SIB = 0
S_X = 1
S_MIX = 7
S_OD = 8
S_W = 10
S_A1 = 42
S_A2 = 50
S_RS = 58
S_E = 70
S_F1 = 78
S_F2 = 85
S_F3 = 88
S_B1 = 95
S_B2 = 102
S_B3 = 105
S_ALL = 112


def dot(a, b):
    return lax.dot_general(a, b, (((1,), (0,)), ((), ())), preferred_element_type=F32)


def dot_t0(a, b):
    return lax.dot_general(a, b, (((0,), (0,)), ((), ())), preferred_element_type=F32)


def dot_t1(a, b):
    return lax.dot_general(a, b, (((1,), (1,)), ((), ())), preferred_element_type=F32)


def kernel(
    q, k, v, ld, gain, w, g,
    dq, dk, dv, dw,
    OG, OGS, WB, ACC, XO, XI, MX, DW, R1, R2, R3, R4, R1B, R2B, E1, E2, E3, E4,
    PB, ATT, DA, DL, CC, RN, CR,
    ST, STI, RT, RTI, EN, ENT, LL, EP,
    GS, GSI, GR, GRI, GO, GG,
    ss, rs,
):
    me = lax.axis_index("seq")
    x = lax.axis_index("head")
    y = lax.div(me, 8)
    grp = lax.rem(me, 8)
    z = lax.div(grp, 2)
    c = lax.rem(me, 2)
    o = 1 - c

    def turn(a, d):
        return lax.rem(a + d, 4)

    yn, yo, yp = turn(y, 1), turn(y, 2), turn(y, 3)
    zn, zo, zp = turn(z, 1), turn(z, 2), turn(z, 3)
    xn, xo, xp = turn(x, 1), turn(x, 2), turn(x, 3)

    def at(yy, zz, cc):
        return ((yy * 4 + zz) * 2 + cc, x)

    YN, YP, ZN, ZP = at(yn, z, c), at(yp, z, c), at(y, zn, c), at(y, zp, c)
    XN, XP = (me, xn), (me, xp)
    SIB = at(y, z, o)

    def mate(d):
        p = lax.rem(grp + d, 8)
        return p, (y * 8 + p, x)

    live = []

    def make(i, src, dst, dev):
        return pltpu.make_async_remote_copy(
            src_ref=src,
            dst_ref=dst,
            send_sem=ss.at[i],
            recv_sem=rs.at[i],
            device_id=dev,
            device_id_type=MESH,
        )

    def put(i, src, dst, dev):
        copy = make(i, src, dst, dev)
        copy.start()
        live.append(copy)
        return copy

    def same(i, ref, dev):
        return put(i, ref, ref, dev)

    barrier = pltpu.get_barrier_semaphore()
    partners = [mate(d)[1] for d in range(1, 8)]
    partners += [at(turn(y, d), z, c) for d in (1, 2, 3)]
    partners += [XN, XP]
    for dev in partners:
        pl.semaphore_signal(barrier, inc=1, device_id=dev, device_id_type=MESH)
    pl.semaphore_wait(barrier, len(partners))

    own_rows = pl.ds(pl.multiple_of(c * ROWS, ROWS), ROWS)
    sib_rows = pl.ds(pl.multiple_of(o * ROWS, ROWS), ROWS)

    half = (pl.ds(0, HALF), pl.ds(HALF, HALF))
    quart = tuple(tuple(pl.ds(a * HALF + b * QUART, QUART) for b in range(2)) for a in range(2))

    WB[y, z] = w[...]
    wy0 = same(S_W + 0, WB.at[y, z], YN)
    wy1 = same(S_W + 1, WB.at[y, z], YP)
    wz0 = same(S_W + 2, WB.at[y, z], ZN)
    wz1 = same(S_W + 3, WB.at[y, z], ZP)

    for part in range(4):
        r = pl.ds(part * 128, 128)
        rows = g[r, :]
        even = jnp.concatenate(
            [rows[:, (2 * i) * UNIT : (2 * i + 1) * UNIT] for i in range(4)], axis=1
        )
        odd = jnp.concatenate(
            [rows[:, (2 * i + 1) * UNIT : (2 * i + 2) * UNIT] for i in range(4)], axis=1
        )
        mine = jnp.where(c == 0, even, odd)
        other = jnp.where(c == 0, odd, even)
        OG[x, pl.ds(pl.multiple_of(c * ROWS + part * 128, 128), 128), :] = mine
        OGS[r, :] = other
    sib = put(S_SIB, OGS, OG.at[x, own_rows], SIB)
    xr0 = put(S_X + 0, OG.at[x, own_rows], OG.at[x, own_rows], XN)
    xl1 = put(S_X + 3, OG.at[x, own_rows], OG.at[x, own_rows], XP)

    row_i = lax.broadcasted_iota(jnp.int32, (ROWS, ROWS), 0)
    col_i = lax.broadcasted_iota(jnp.int32, (ROWS, ROWS), 1)
    upper = (row_i <= col_i).astype(F32)
    lower = (row_i >= col_i).astype(F32)
    by_rows = lax.dot_general(
        ld[...], upper, (((1,), (0,)), ((), ())), precision=HIGH, preferred_element_type=F32
    )
    by_cols = lax.dot_general(
        lower, ld[...], (((1,), (1,)), ((), ())), precision=HIGH, preferred_element_type=F32
    )
    for h in range(HEADS):
        CR[h] = by_rows[h : h + 1, :]
        CC[h] = jnp.broadcast_to(by_cols[:, h : h + 1], (ROWS, WIDE))

    sib.wait_recv()
    xl0 = put(S_X + 2, OG.at[x, sib_rows], OG.at[x, sib_rows], XP)
    xr1 = put(S_X + 1, OG.at[x, sib_rows], OG.at[x, sib_rows], XN)

    def head_cols(h):
        return pl.ds(pl.multiple_of(h * WIDE, WIDE), WIDE)

    def decays(h, tb, sb):
        cc = CC[h, pl.ds(tb * BLK, BLK), :]
        cr = CR[h, :, pl.ds(sb * BLK, BLK)]
        grown = jnp.exp(jnp.concatenate([cc, cc], axis=1) - cr)
        if tb == sb:
            t = lax.broadcasted_iota(jnp.int32, (BLK, BLK), 0)
            s = lax.broadcasted_iota(jnp.int32, (BLK, BLK), 1)
            grown = jnp.where(t >= s, grown, 0.0)
        return grown

    def blk(b):
        return pl.ds(b * BLK, BLK)

    row16 = lax.broadcasted_iota(jnp.int32, (16, WIDE), 0)

    def split3(row):
        hi = row.astype(BF).astype(F32)
        mid = (row - hi).astype(BF).astype(F32)
        lo = (row - hi - mid).astype(BF).astype(F32)
        full = jnp.where(
            row16 == 0, hi, jnp.where(row16 == 1, mid, jnp.where(row16 == 2, lo, 0.0))
        )
        return full.astype(BF)

    def join3(block):
        return jnp.sum(block.astype(F32), axis=0, keepdims=True)

    def forward_head(h):
        hs = head_cols(h)
        for tb in range(2):
            out = jnp.zeros((BLK, WIDE), F32)
            for sb in range(tb + 1):
                scores = dot_t1(q[blk(tb), hs], k[blk(sb), hs])
                p = (scores * decays(h, tb, sb)).astype(BF)
                PB[h, blk(tb), blk(sb)] = p
                out = out + dot(p, v[blk(sb), hs])
            ATT[blk(tb), hs] = out
        total = CR[h, :, pl.ds(ROWS - WIDE, WIDE)][:, WIDE - 1 : WIDE]
        kd = (k[:, hs].astype(F32) * jnp.exp(total - CC[h])).astype(BF)
        ST[h, pl.ds(0, WIDE), :] = dot_t0(kd, v[:, hs]).astype(BF)
        ST[h, pl.ds(WIDE, 16), :] = split3(jnp.broadcast_to(total, (1, WIDE)))

    def first(d):
        p, dev = mate(d)
        return make(S_F1 + d - 1, ST.at[p], STI.at[grp], dev)

    def forward_step(d, _):
        forward_head(lax.rem(grp + d, 8))
        first(d).start()
        return 0

    lax.fori_loop(1, 8, forward_step, 0)
    forward_head(grp)
    STI[grp] = ST[grp]
    f1 = [first(d) for d in range(1, 8)]
    live += f1

    wy0.wait_recv()
    wyf0 = same(S_W + 4, WB.at[yp, z, half[0]], YN)
    wyp0 = same(S_W + 5, WB.at[yp, z, half[0]], ZN)
    wyp1 = same(S_W + 6, WB.at[yp, z, half[0]], ZP)
    wy1.wait_recv()
    wyf1 = same(S_W + 7, WB.at[yn, z, half[1]], YP)
    wyn0 = same(S_W + 8, WB.at[yn, z, half[0]], ZN)
    wyn1 = same(S_W + 9, WB.at[yn, z, half[0]], ZP)
    wz0.wait_recv()
    wzf0 = same(S_W + 10, WB.at[y, zp, half[0]], ZN)
    wzp0 = same(S_W + 11, WB.at[y, zp, half[1]], YN)
    wzp1 = same(S_W + 12, WB.at[y, zp, half[1]], YP)
    wz1.wait_recv()
    wzf1 = same(S_W + 13, WB.at[y, zn, half[1]], ZP)
    wzn0 = same(S_W + 14, WB.at[y, zn, half[1]], YN)
    wzn1 = same(S_W + 15, WB.at[y, zn, half[1]], YP)

    for copy in f1:
        copy.wait_recv()

    def chain(i, carry):
        state, logs = carry
        log_i = join3(STI[i, pl.ds(WIDE, 16), :])
        LL[i] = state
        EP[i] = logs
        state = jnp.exp(log_i) * state + STI[i, pl.ds(0, WIDE), :].astype(F32)
        return state, logs + log_i

    row_state, row_logs = lax.fori_loop(
        0, 8, chain, (jnp.zeros((WIDE, WIDE), F32), jnp.zeros((1, WIDE), F32))
    )
    RT[pl.ds(0, WIDE), :] = row_state.astype(BF)
    RT[pl.ds(WIDE, 16), :] = split3(row_logs)
    RTI[y] = RT[...]
    f2 = [
        put(S_F2 + d - 1, RT, RTI.at[y], at(turn(y, d), z, c)) for d in (1, 2, 3)
    ]
    for copy in f2:
        copy.wait_recv()
    carried = jnp.zeros((WIDE, WIDE), F32)
    for yy in range(3):
        grown = jnp.exp(join3(RTI[yy, pl.ds(WIDE, 16), :])) * carried
        grown = grown + RTI[yy, pl.ds(0, WIDE), :].astype(F32)
        carried = jnp.where(yy < y, grown, carried)

    def enter(i, _):
        EN[i] = (LL[i] + jnp.exp(EP[i]) * carried).astype(BF)
        return 0

    lax.fori_loop(0, 8, enter, 0)
    ENT[grp] = EN[grp]
    f3 = []
    for d in range(1, 8):
        p, dev = mate(d)
        f3.append(put(S_F3 + d - 1, EN.at[p], ENT.at[grp], dev))

    wyf0.wait_recv()
    wyf1.wait_recv()
    wyo0 = same(S_W + 16, WB.at[yo, z, half[0]], ZN)
    wyo1 = same(S_W + 17, WB.at[yo, z, half[0]], ZP)
    wzf0.wait_recv()
    wzf1.wait_recv()
    wzo0 = same(S_W + 18, WB.at[y, zo, half[1]], YN)
    wzo1 = same(S_W + 19, WB.at[y, zo, half[1]], YP)
    w3 = []
    for i, (copy, ref, dev) in enumerate(
        (
            (wyp0, WB.at[yp, zp, quart[0][0]], ZN),
            (wyp1, WB.at[yp, zn, quart[0][1]], ZP),
            (wzp0, WB.at[yp, zp, quart[1][0]], YN),
            (wzp1, WB.at[yn, zp, quart[1][1]], YP),
            (wyn0, WB.at[yn, zp, quart[0][0]], ZN),
            (wyn1, WB.at[yn, zn, quart[0][1]], ZP),
            (wzn0, WB.at[yp, zn, quart[1][0]], YN),
            (wzn1, WB.at[yn, zn, quart[1][1]], YP),
        )
    ):
        copy.wait_recv()
        w3.append(same(S_W + 20 + i, ref, dev))

    for copy in f3:
        copy.wait_recv()

    mean_of = jnp.full((WIDE, WIDE), 1.0 / WIDE, BF)

    def halves(a):
        high = a.astype(BF)
        return high, (a - high.astype(F32)).astype(BF)

    def row_mean(a):
        high, low = halves(a)
        return dot(high, mean_of) + dot(low, mean_of)

    def attend_head(h, _):
        hs = head_cols(h)
        att = ATT[:, hs] + jnp.exp(CC[h]) * dot(q[:, hs], ENT[h])
        r = lax.rsqrt(row_mean(att * att) + EPSILON)
        scaled = att * r
        ATT[:, hs] = scaled
        RN[h] = r
        MX[c, :, hs] = (scaled * gain[:, hs]).astype(BF)
        return 0

    lax.fori_loop(0, HEADS, attend_head, 0)
    mix = put(S_MIX, MX.at[c], MX.at[c], SIB)

    for i, (copy, ref, dev) in enumerate(
        (
            (wyo0, WB.at[yo, zp, quart[0][0]], ZN),
            (wyo1, WB.at[yo, zn, quart[0][1]], ZP),
            (wzo0, WB.at[yp, zo, quart[1][0]], YN),
            (wzo1, WB.at[yn, zo, quart[1][1]], YP),
        )
    ):
        copy.wait_recv()
        w3.append(same(S_W + 28 + i, ref, dev))

    def weight_term(xx):
        def tile(i, _):
            pair = lax.div(i, 2)
            n = lax.rem(i, 2)
            ms = pl.ds(pl.multiple_of(pair * 384, 384), 384)
            ns = pl.ds(pl.multiple_of(n * 512, 512), 512)
            term = dot_t0(OG[xx, pl.ds(0, ROWS), ms], MX[0, :, ns])
            term = term + dot_t0(OG[xx, pl.ds(ROWS, ROWS), ms], MX[1, :, ns])
            DW[xx, pl.ds(2 * pair, 2), :, ns] = term.reshape(2, UNIT, 512).astype(BF)
            return 0

        lax.fori_loop(0, 4, tile, 0)

    def delta_term(xx, first, half):
        def tile(n, _):
            ms = pl.ds(pl.multiple_of(half * ROWS, ROWS), ROWS)
            ns = pl.ds(pl.multiple_of(n * 256, 256), 256)
            term = dot(OG[xx, ms, :], WB[xx, :, :, ns].reshape(SPAN, 256))
            if first:
                ACC[ms, ns] = term
            else:
                ACC[ms, ns] += term
            return 0

        lax.fori_loop(0, 4, tile, 0)

    def add_to(target, *more):
        total = target.astype(F32)
        for term in more:
            total = total + term.astype(F32)
        return total.astype(BF)

    early = ((0, x), (1, xp), (2, xn))
    b1lo = make(S_RS + 0, DW.at[yo, :, quart[1][0]], R1B.at[0], YN)
    b1hi = make(S_RS + 1, DW.at[yo, :, quart[1][1]], R1B.at[1], YP)
    b2n = make(S_RS + 2, DW.at[yn, :, half[1]], R2B.at[0], YN)
    b2p = make(S_RS + 3, DW.at[yp, :, half[1]], R2B.at[1], YP)
    c1lo = make(S_RS + 4, DW.at[yo, z, quart[0][0]], R3.at[0, 0], YN)
    c1hi = make(S_RS + 5, DW.at[yo, z, quart[0][1]], R3.at[0, 1], YP)
    c2n = make(S_RS + 6, DW.at[yn, z, half[0]], R4.at[0, 0], YN)
    c2p = make(S_RS + 7, DW.at[yp, z, half[0]], R4.at[0, 1], YP)
    d1lo = make(S_RS + 8, DW.at[y, zo, quart[1][0]], R3.at[1, 0], ZN)
    d1hi = make(S_RS + 9, DW.at[y, zo, quart[1][1]], R3.at[1, 1], ZP)
    d2n = make(S_RS + 10, DW.at[y, zn, half[1]], R4.at[1, 0], ZN)
    d2p = make(S_RS + 11, DW.at[y, zp, half[1]], R4.at[1, 1], ZP)
    e1lo = make(S_E + 0, DW.at[xo, zo, half[0]], E1.at[0], ZN)
    e1hi = make(S_E + 1, DW.at[xo, zo, half[1]], E1.at[1], ZP)
    e2n = make(S_E + 2, DW.at[xo, zn], E2.at[0], ZN)
    e2p = make(S_E + 3, DW.at[xo, zp], E2.at[1], ZP)
    f1lo = make(S_E + 4, DW.at[xo, z, half[0]], E3.at[0], YN)
    f1hi = make(S_E + 5, DW.at[xo, z, half[1]], E3.at[1], YP)
    f2n = make(S_E + 6, DW.at[xo, z], E4.at[0], YN)
    f2p = make(S_E + 7, DW.at[xo, z], E4.at[1], YP)
    live += [e1lo, e1hi, e2n, e2p]
    a1 = {}
    a2 = {}

    def first_hop(j, xx):
        a1[j] = (
            put(S_A1 + 2 * j, DW.at[xx, zo, quart[0][0]], R1.at[0, j], ZN),
            put(S_A1 + 2 * j + 1, DW.at[xx, zo, quart[0][1]], R1.at[1, j], ZP),
        )

    def first_hop_y():
        @pl.when(yo != xo)
        def _():
            b1lo.start()
            b1hi.start()

    def second_hop():
        for j, xx in early:
            a1[j][0].wait_recv()
            DW[xx, zn, quart[0][0]] = add_to(DW[xx, zn, quart[0][0]], R1[0, j])
            to_n = put(S_A2 + 2 * j, DW.at[xx, zn, half[0]], R2.at[0, j], ZN)
            a1[j][1].wait_recv()
            DW[xx, zp, quart[0][1]] = add_to(DW[xx, zp, quart[0][1]], R1[1, j])
            to_p = put(S_A2 + 2 * j + 1, DW.at[xx, zp, half[0]], R2.at[1, j], ZP)
            a2[j] = (to_n, to_p)

        @pl.when(yn != xo)
        def _():
            b1lo.wait_recv()
            for i in range(4):
                DW[yn, i, quart[1][0]] = add_to(DW[yn, i, quart[1][0]], R1B[0, i])
            b2n.start()

        @pl.when(yp != xo)
        def _():
            b1hi.wait_recv()
            for i in range(4):
                DW[yp, i, quart[1][1]] = add_to(DW[yp, i, quart[1][1]], R1B[1, i])
            b2p.start()

    def third_hop():
        for j, xx in early:
            a2[j][0].wait_recv()
            a2[j][1].wait_recv()
            DW[xx, z, half[0]] = add_to(DW[xx, z, half[0]], R2[0, j], R2[1, j])

        @pl.when(yo != xo)
        def _():
            c1lo.start()
            c1hi.start()

        @pl.when(y != xo)
        def _():
            b2n.wait_recv()
            b2p.wait_recv()
            for i in range(4):
                DW[y, i, half[1]] = add_to(DW[y, i, half[1]], R2B[0, i], R2B[1, i])
            d1lo.start()
            d1hi.start()

    def fourth_hop():
        @pl.when(yn != xo)
        def _():
            c1lo.wait_recv()
            DW[yn, z, quart[0][0]] = add_to(DW[yn, z, quart[0][0]], R3[0, 0])
            c2n.start()

        @pl.when(yp != xo)
        def _():
            c1hi.wait_recv()
            DW[yp, z, quart[0][1]] = add_to(DW[yp, z, quart[0][1]], R3[0, 1])
            c2p.start()

        @pl.when(y != xo)
        def _():
            d1lo.wait_recv()
            DW[y, zn, quart[1][0]] = add_to(DW[y, zn, quart[1][0]], R3[1, 0])
            d2n.start()
            d1hi.wait_recv()
            DW[y, zp, quart[1][1]] = add_to(DW[y, zp, quart[1][1]], R3[1, 1])
            d2p.start()

    def late_second_hop():
        e1lo.wait_recv()
        DW[xo, zn, half[0]] = add_to(DW[xo, zn, half[0]], E1[0])
        e2n.start()
        e1hi.wait_recv()
        DW[xo, zp, half[1]] = add_to(DW[xo, zp, half[1]], E1[1])
        e2p.start()

    def late_third_hop():
        e2n.wait_recv()
        e2p.wait_recv()
        for i in range(2):
            DW[xo, z, half[i]] = add_to(DW[xo, z, half[i]], E2[0, half[i]], E2[1, half[i]])

        @pl.when(yo == xo)
        def _():
            f1lo.start()
            f1hi.start()

    def late_fourth_hop():
        @pl.when(yn == xo)
        def _():
            f1lo.wait_recv()
            DW[xo, z, half[0]] = add_to(DW[xo, z, half[0]], E3[0])
            f2n.start()

        @pl.when(yp == xo)
        def _():
            f1hi.wait_recv()
            DW[xo, z, half[1]] = add_to(DW[xo, z, half[1]], E3[1])
            f2p.start()

    mix.wait_recv()
    weight_term(x)
    first_hop(0, x)

    xr0.wait_recv()
    xr2 = put(S_X + 4, OG.at[xp, own_rows], OG.at[xp, own_rows], XN)
    xl0.wait_recv()
    xl2 = put(S_X + 5, OG.at[xn, sib_rows], OG.at[xn, sib_rows], XP)
    xr1.wait_recv()
    weight_term(xp)
    first_hop(1, xp)
    xl1.wait_recv()
    weight_term(xn)
    first_hop(2, xn)
    first_hop_y()

    for copy in w3:
        copy.wait_recv()
    delta_term(x, True, o)
    delta_term(x, True, c)
    delta_term(xp, False, o)
    delta_term(xp, False, c)
    second_hop()
    delta_term(xn, False, o)
    delta_term(xn, False, c)
    xr2.wait_recv()
    xl2.wait_recv()

    weight_term(xo)
    e1lo.start()
    e1hi.start()
    ods = []
    for m in range(2):

        def last_tile(n, _):
            ns = pl.ds(pl.multiple_of(n * 256, 256), 256)
            term = dot(OG[xo, sib_rows, :], WB[xo, :, :, ns].reshape(SPAN, 256))
            XO[:, ns] = (ACC[sib_rows, ns] + term).astype(BF)
            return 0

        lax.fori_loop(2 * m, 2 * m + 2, last_tile, 0)
        part = pl.ds(m * ROWS, ROWS)
        ods.append(put(S_OD + m, XO.at[:, part], XI.at[:, part], SIB))
    delta_term(xo, False, c)
    for copy in ods:
        copy.wait_recv()

    def norm_back_head(h):
        hs = head_cols(h)
        delta = ACC[own_rows, hs] + XI[:, hs].astype(F32)
        scaled = ATT[:, hs]
        gg = delta * gain[:, hs]
        da = RN[h] * (gg - scaled * row_mean(gg * scaled))
        da, low = halves(da)
        DA[:, hs] = da
        DL[:, hs] = low
        qd = (q[:, hs].astype(F32) * jnp.exp(CC[h])).astype(BF)
        GS[h] = dot_t0(qd, da).astype(BF)

    def first_back(d):
        p, dev = mate(d)
        return make(S_B1 + d - 1, GS.at[p], GSI.at[grp], dev)

    def norm_back_step(d, _):
        norm_back_head(lax.rem(grp + d, 8))
        first_back(d).start()
        return 0

    lax.fori_loop(1, 8, norm_back_step, 0)
    norm_back_head(grp)
    GSI[grp] = GS[grp]
    b1 = [first_back(d) for d in range(1, 8)]
    live += b1

    late_second_hop()
    for copy in b1:
        copy.wait_recv()

    def chain_back(n, carry):
        i = 7 - n
        state, logs = carry
        log_i = join3(STI[i, pl.ds(WIDE, 16), :])
        LL[i] = state
        EP[i] = logs
        state = jnp.exp(log_i) * state + GSI[i].astype(F32)
        return state, logs + log_i

    row_back, _ = lax.fori_loop(
        0, 8, chain_back, (jnp.zeros((WIDE, WIDE), F32), jnp.zeros((1, WIDE), F32))
    )
    GR[...] = row_back.astype(BF)
    GRI[y] = GR[...]
    b2 = [
        put(S_B2 + d - 1, GR, GRI.at[y], at(turn(y, d), z, c)) for d in (1, 2, 3)
    ]

    def local_back_head(h, _):
        hs = head_cols(h)
        dk_blk = [None, None]
        dv_blk = [None, None]
        for tb in range(2):
            da = DA[blk(tb), hs]
            out = jnp.exp(CC[h, blk(tb), :]) * dot_t1(da, ENT[h])
            for sb in range(tb + 1):
                vs = v[blk(sb), hs]
                dp = dot_t1(da, vs) + dot_t1(DL[blk(tb), hs], vs)
                dp = (dp * decays(h, tb, sb)).astype(BF)
                out = out + dot(dp, k[blk(sb), hs])
                k_term = dot_t0(dp, q[blk(tb), hs])
                v_term = dot_t0(PB[h, blk(tb), blk(sb)], da)
                dk_blk[sb] = k_term if dk_blk[sb] is None else dk_blk[sb] + k_term
                dv_blk[sb] = v_term if dv_blk[sb] is None else dv_blk[sb] + v_term
            dq[blk(tb), hs] = out.astype(BF)
        for sb in range(2):
            ACC[blk(sb), hs] = dk_blk[sb]
            ACC[blk(2 + sb), hs] = dv_blk[sb]
        return 0

    lax.fori_loop(0, 4, local_back_head, 0)

    third_hop()
    for copy in b2:
        copy.wait_recv()
    carried_back = jnp.zeros((WIDE, WIDE), F32)
    for yy in (3, 2, 1):
        grown = jnp.exp(join3(RTI[yy, pl.ds(WIDE, 16), :])) * carried_back
        grown = grown + GRI[yy].astype(F32)
        carried_back = jnp.where(yy > y, grown, carried_back)

    def leave(i, _):
        GO[i] = (LL[i] + jnp.exp(EP[i]) * carried_back).astype(BF)
        return 0

    lax.fori_loop(0, 8, leave, 0)
    GG[grp] = GO[grp]
    b3 = []
    for d in range(1, 8):
        p, dev = mate(d)
        b3.append(put(S_B3 + d - 1, GO.at[p], GG.at[grp], dev))

    late_third_hop()
    lax.fori_loop(4, 8, local_back_head, 0)

    def last_head(h):
        hs = head_cols(h)
        total = CR[h, :, pl.ds(ROWS - WIDE, WIDE)][:, WIDE - 1 : WIDE]
        tail = jnp.exp(total - CC[h])
        dk[:, hs] = (ACC[pl.ds(0, ROWS), hs] + tail * dot_t1(v[:, hs], GG[h])).astype(BF)
        dv[:, hs] = (ACC[pl.ds(ROWS, ROWS), hs] + tail * dot(k[:, hs], GG[h])).astype(BF)

    fourth_hop()
    last_head(grp)

    def last_step(d, _):
        p = lax.rem(grp + 8 - d, 8)
        make(S_B3 + d - 1, GO.at[p], GG.at[grp], SIB).wait_recv()
        last_head(p)
        return 0

    late_fourth_hop()
    lax.fori_loop(1, 4, last_step, 0)
    lax.fori_loop(4, 8, last_step, 0)

    @pl.when(y != xo)
    def _():
        for i, (from_p, from_n) in enumerate(((c2n, c2p), (d2n, d2p))):
            from_p.wait_recv()
            from_n.wait_recv()
            dw[half[i], :] = (
                DW[y, z, half[i]].astype(F32) + R4[i, 0].astype(F32) + R4[i, 1].astype(F32)
            ) * SCALE

    @pl.when(y == xo)
    def _():
        f2n.wait_recv()
        f2p.wait_recv()
        for i in range(2):
            dw[half[i], :] = (
                DW[y, z, half[i]].astype(F32)
                + E4[0, half[i]].astype(F32)
                + E4[1, half[i]].astype(F32)
            ) * SCALE

    for place, copies in (
        (yo, (b1lo, b1hi, c1lo, c1hi)),
        (yn, (b2n, c2n)),
        (yp, (b2p, c2p)),
        (y, (d1lo, d1hi, d2n, d2p)),
    ):

        @pl.when(place != xo)
        def _():
            for copy in copies:
                copy.wait_send()

    for place, copies in ((yo, (f1lo, f1hi)), (yn, (f2n,)), (yp, (f2p,))):

        @pl.when(place == xo)
        def _():
            for copy in copies:
                copy.wait_send()

    for copy in live:
        copy.wait_send()


def body(query_rows, key_rows, value_rows, log_decay, norm_gain, out_weight, out_grad):
    vm = pltpu.VMEM
    scratch = [
        vm((4, 2 * ROWS, SPAN), BF),
        vm((ROWS, SPAN), BF),
        vm((4, 4, UNIT, COLS), BF),
        vm((2 * ROWS, COLS), F32),
        vm((ROWS, COLS), BF),
        vm((ROWS, COLS), BF),
        vm((2, ROWS, COLS), BF),
        vm((4, 4, UNIT, COLS), BF),
        vm((2, 3, QUART, COLS), BF),
        vm((2, 3, HALF, COLS), BF),
        vm((2, 2, QUART, COLS), BF),
        vm((2, 2, HALF, COLS), BF),
        vm((2, 4, QUART, COLS), BF),
        vm((2, 4, HALF, COLS), BF),
        vm((2, HALF, COLS), BF),
        vm((2, UNIT, COLS), BF),
        vm((2, HALF, COLS), BF),
        vm((2, UNIT, COLS), BF),
        vm((HEADS, ROWS, ROWS), BF),
        vm((ROWS, COLS), F32),
        vm((ROWS, COLS), BF),
        vm((ROWS, COLS), BF),
        vm((HEADS, ROWS, WIDE), F32),
        vm((HEADS, ROWS, WIDE), F32),
        vm((HEADS, 1, ROWS), F32),
        vm((8, WIDE + 16, WIDE), BF),
        vm((8, WIDE + 16, WIDE), BF),
        vm((WIDE + 16, WIDE), BF),
        vm((4, WIDE + 16, WIDE), BF),
        vm((8, WIDE, WIDE), BF),
        vm((8, WIDE, WIDE), BF),
        vm((8, WIDE, WIDE), F32),
        vm((8, 1, WIDE), F32),
        vm((8, WIDE, WIDE), BF),
        vm((8, WIDE, WIDE), BF),
        vm((WIDE, WIDE), BF),
        vm((4, WIDE, WIDE), BF),
        vm((8, WIDE, WIDE), BF),
        vm((8, WIDE, WIDE), BF),
        pltpu.SemaphoreType.DMA((S_ALL,)),
        pltpu.SemaphoreType.DMA((S_ALL,)),
    ]
    spec = pl.BlockSpec(memory_space=pltpu.VMEM)
    shapes = (
        jax.ShapeDtypeStruct((ROWS, COLS), BF),
        jax.ShapeDtypeStruct((ROWS, COLS), BF),
        jax.ShapeDtypeStruct((ROWS, COLS), BF),
        jax.ShapeDtypeStruct((UNIT, COLS), F32),
    )
    return pl.pallas_call(
        kernel,
        out_shape=shapes,
        in_specs=[spec] * 7,
        out_specs=(spec,) * 4,
        scratch_shapes=scratch,
        compiler_params=pltpu.CompilerParams(
            collective_id=0, has_side_effects=True, vmem_limit_bytes=62 * 2**20
        ),
    )(
        query_rows,
        key_rows,
        value_rows,
        log_decay,
        norm_gain.reshape(1, COLS),
        out_weight,
        out_grad,
    )


def solution(mesh):
    both = P("seq", "head")
    return jax.shard_map(
        body,
        mesh=mesh,
        in_specs=(both, both, both, P("head", "seq"), P("head"), both, both),
        out_specs=(both, both, both, both),
        check_vma=False,
    )
```

```python
import jax
import jax.numpy as jnp
from jax import lax
from jax.experimental import pallas as pl
from jax.experimental.pallas import tpu as pltpu
from jax.sharding import PartitionSpec as P

MESH = pl.DeviceIdType.MESH
BF = jnp.bfloat16
F32 = jnp.float32
HIGH = lax.Precision.HIGHEST
EPSILON = 1e-06

ROWS = 512
HEADS = 8
WIDE = 128
COLS = 1024
UNIT = 192
HALF = 96
QUART = 48
SPAN = 768
BLK = 256
SCALE = 1.0 / 128.0

S_SIB = 0
S_X = 1
S_MIX = 7
S_OD = 8
S_W = 10
S_A1 = 42
S_A2 = 50
S_RS = 58
S_E = 70
S_F1 = 78
S_F2 = 85
S_F3 = 88
S_B1 = 95
S_B2 = 102
S_B3 = 105
S_ALL = 112


def dot(a, b):
    return lax.dot_general(a, b, (((1,), (0,)), ((), ())), preferred_element_type=F32)


def dot_t0(a, b):
    return lax.dot_general(a, b, (((0,), (0,)), ((), ())), preferred_element_type=F32)


def dot_t1(a, b):
    return lax.dot_general(a, b, (((1,), (1,)), ((), ())), preferred_element_type=F32)


def kernel(
    q, k, v, ld, gain, w, g,
    dq, dk, dv, dw,
    OG, OGS, WB, ACC, XO, XI, MX, DW, R1, R2, R3, R4, R1B, R2B, E1, E2, E3, E4,
    PB, ATT, DA, DL, CC, RN, CR,
    ST, STI, RT, RTI, EN, ENT, LL, EP,
    GS, GSI, GR, GRI, GO, GG,
    ss, rs,
):
    me = lax.axis_index("seq")
    x = lax.axis_index("head")
    y = lax.div(me, 8)
    grp = lax.rem(me, 8)
    z = lax.div(grp, 2)
    c = lax.rem(me, 2)
    o = 1 - c

    def turn(a, d):
        return lax.rem(a + d, 4)

    yn, yo, yp = turn(y, 1), turn(y, 2), turn(y, 3)
    zn, zo, zp = turn(z, 1), turn(z, 2), turn(z, 3)
    xn, xo, xp = turn(x, 1), turn(x, 2), turn(x, 3)

    def at(yy, zz, cc):
        return ((yy * 4 + zz) * 2 + cc, x)

    YN, YP, ZN, ZP = at(yn, z, c), at(yp, z, c), at(y, zn, c), at(y, zp, c)
    XN, XP = (me, xn), (me, xp)
    SIB = at(y, z, o)

    def mate(d):
        p = lax.rem(grp + d, 8)
        return p, (y * 8 + p, x)

    live = []

    def make(i, src, dst, dev):
        return pltpu.make_async_remote_copy(
            src_ref=src,
            dst_ref=dst,
            send_sem=ss.at[i],
            recv_sem=rs.at[i],
            device_id=dev,
            device_id_type=MESH,
        )

    def put(i, src, dst, dev):
        copy = make(i, src, dst, dev)
        copy.start()
        live.append(copy)
        return copy

    def same(i, ref, dev):
        return put(i, ref, ref, dev)

    barrier = pltpu.get_barrier_semaphore()
    partners = [mate(d)[1] for d in range(1, 8)]
    partners += [at(turn(y, d), z, c) for d in (1, 2, 3)]
    partners += [XN, XP]
    for dev in partners:
        pl.semaphore_signal(barrier, inc=1, device_id=dev, device_id_type=MESH)
    pl.semaphore_wait(barrier, len(partners))

    own_rows = pl.ds(pl.multiple_of(c * ROWS, ROWS), ROWS)
    sib_rows = pl.ds(pl.multiple_of(o * ROWS, ROWS), ROWS)

    half = (pl.ds(0, HALF), pl.ds(HALF, HALF))
    quart = tuple(tuple(pl.ds(a * HALF + b * QUART, QUART) for b in range(2)) for a in range(2))

    WB[y, z] = w[...]
    wy0 = same(S_W + 0, WB.at[y, z], YN)
    wy1 = same(S_W + 1, WB.at[y, z], YP)
    wz0 = same(S_W + 2, WB.at[y, z], ZN)
    wz1 = same(S_W + 3, WB.at[y, z], ZP)

    for part in range(4):
        r = pl.ds(part * 128, 128)
        rows = g[r, :]
        even = jnp.concatenate(
            [rows[:, (2 * i) * UNIT : (2 * i + 1) * UNIT] for i in range(4)], axis=1
        )
        odd = jnp.concatenate(
            [rows[:, (2 * i + 1) * UNIT : (2 * i + 2) * UNIT] for i in range(4)], axis=1
        )
        mine = jnp.where(c == 0, even, odd)
        other = jnp.where(c == 0, odd, even)
        OG[x, pl.ds(pl.multiple_of(c * ROWS + part * 128, 128), 128), :] = mine
        OGS[r, :] = other
    sib = put(S_SIB, OGS, OG.at[x, own_rows], SIB)
    xr0 = put(S_X + 0, OG.at[x, own_rows], OG.at[x, own_rows], XN)
    xl1 = put(S_X + 3, OG.at[x, own_rows], OG.at[x, own_rows], XP)

    row_i = lax.broadcasted_iota(jnp.int32, (ROWS, ROWS), 0)
    col_i = lax.broadcasted_iota(jnp.int32, (ROWS, ROWS), 1)
    upper = (row_i <= col_i).astype(F32)
    lower = (row_i >= col_i).astype(F32)
    by_rows = lax.dot_general(
        ld[...], upper, (((1,), (0,)), ((), ())), precision=HIGH, preferred_element_type=F32
    )
    by_cols = lax.dot_general(
        lower, ld[...], (((1,), (1,)), ((), ())), precision=HIGH, preferred_element_type=F32
    )
    for h in range(HEADS):
        CR[h] = by_rows[h : h + 1, :]
        CC[h] = jnp.broadcast_to(by_cols[:, h : h + 1], (ROWS, WIDE))

    sib.wait_recv()
    xl0 = put(S_X + 2, OG.at[x, sib_rows], OG.at[x, sib_rows], XP)
    xr1 = put(S_X + 1, OG.at[x, sib_rows], OG.at[x, sib_rows], XN)

    def head_cols(h):
        return pl.ds(pl.multiple_of(h * WIDE, WIDE), WIDE)

    def decays(h, tb, sb):
        cc = CC[h, pl.ds(tb * BLK, BLK), :]
        cr = CR[h, :, pl.ds(sb * BLK, BLK)]
        grown = jnp.exp(jnp.concatenate([cc, cc], axis=1) - cr)
        if tb == sb:
            t = lax.broadcasted_iota(jnp.int32, (BLK, BLK), 0)
            s = lax.broadcasted_iota(jnp.int32, (BLK, BLK), 1)
            grown = jnp.where(t >= s, grown, 0.0)
        return grown

    def blk(b):
        return pl.ds(b * BLK, BLK)

    row16 = lax.broadcasted_iota(jnp.int32, (16, WIDE), 0)

    def split3(row):
        hi = row.astype(BF).astype(F32)
        mid = (row - hi).astype(BF).astype(F32)
        lo = (row - hi - mid).astype(BF).astype(F32)
        full = jnp.where(
            row16 == 0, hi, jnp.where(row16 == 1, mid, jnp.where(row16 == 2, lo, 0.0))
        )
        return full.astype(BF)

    def join3(block):
        return jnp.sum(block.astype(F32), axis=0, keepdims=True)

    def forward_head(h):
        hs = head_cols(h)
        for tb in range(2):
            out = jnp.zeros((BLK, WIDE), F32)
            for sb in range(tb + 1):
                scores = dot_t1(q[blk(tb), hs], k[blk(sb), hs])
                p = (scores * decays(h, tb, sb)).astype(BF)
                PB[h, blk(tb), blk(sb)] = p
                out = out + dot(p, v[blk(sb), hs])
            ATT[blk(tb), hs] = out
        total = CR[h, :, pl.ds(ROWS - WIDE, WIDE)][:, WIDE - 1 : WIDE]
        kd = (k[:, hs].astype(F32) * jnp.exp(total - CC[h])).astype(BF)
        ST[h, pl.ds(0, WIDE), :] = dot_t0(kd, v[:, hs]).astype(BF)
        ST[h, pl.ds(WIDE, 16), :] = split3(jnp.broadcast_to(total, (1, WIDE)))

    def first(d):
        p, dev = mate(d)
        return make(S_F1 + d - 1, ST.at[p], STI.at[grp], dev)

    def forward_step(d, _):
        forward_head(lax.rem(grp + d, 8))
        first(d).start()
        return 0

    lax.fori_loop(1, 8, forward_step, 0)
    forward_head(grp)
    STI[grp] = ST[grp]
    f1 = [first(d) for d in range(1, 8)]
    live += f1

    wy0.wait_recv()
    wyf0 = same(S_W + 4, WB.at[yp, z, half[0]], YN)
    wyp0 = same(S_W + 5, WB.at[yp, z, half[0]], ZN)
    wyp1 = same(S_W + 6, WB.at[yp, z, half[0]], ZP)
    wy1.wait_recv()
    wyf1 = same(S_W + 7, WB.at[yn, z, half[1]], YP)
    wyn0 = same(S_W + 8, WB.at[yn, z, half[0]], ZN)
    wyn1 = same(S_W + 9, WB.at[yn, z, half[0]], ZP)
    wz0.wait_recv()
    wzf0 = same(S_W + 10, WB.at[y, zp, half[0]], ZN)
    wzp0 = same(S_W + 11, WB.at[y, zp, half[1]], YN)
    wzp1 = same(S_W + 12, WB.at[y, zp, half[1]], YP)
    wz1.wait_recv()
    wzf1 = same(S_W + 13, WB.at[y, zn, half[1]], ZP)
    wzn0 = same(S_W + 14, WB.at[y, zn, half[1]], YN)
    wzn1 = same(S_W + 15, WB.at[y, zn, half[1]], YP)

    for copy in f1:
        copy.wait_recv()

    def chain(i, carry):
        state, logs = carry
        log_i = join3(STI[i, pl.ds(WIDE, 16), :])
        LL[i] = state
        EP[i] = logs
        state = jnp.exp(log_i) * state + STI[i, pl.ds(0, WIDE), :].astype(F32)
        return state, logs + log_i

    row_state, row_logs = lax.fori_loop(
        0, 8, chain, (jnp.zeros((WIDE, WIDE), F32), jnp.zeros((1, WIDE), F32))
    )
    RT[pl.ds(0, WIDE), :] = row_state.astype(BF)
    RT[pl.ds(WIDE, 16), :] = split3(row_logs)
    RTI[y] = RT[...]
    f2 = [
        put(S_F2 + d - 1, RT, RTI.at[y], at(turn(y, d), z, c)) for d in (1, 2, 3)
    ]
    for copy in f2:
        copy.wait_recv()
    carried = jnp.zeros((WIDE, WIDE), F32)
    for yy in range(3):
        grown = jnp.exp(join3(RTI[yy, pl.ds(WIDE, 16), :])) * carried
        grown = grown + RTI[yy, pl.ds(0, WIDE), :].astype(F32)
        carried = jnp.where(yy < y, grown, carried)

    def enter(i, _):
        EN[i] = (LL[i] + jnp.exp(EP[i]) * carried).astype(BF)
        return 0

    lax.fori_loop(0, 8, enter, 0)
    ENT[grp] = EN[grp]
    f3 = []
    for d in range(1, 8):
        p, dev = mate(d)
        f3.append(put(S_F3 + d - 1, EN.at[p], ENT.at[grp], dev))

    wyf0.wait_recv()
    wyf1.wait_recv()
    wyo0 = same(S_W + 16, WB.at[yo, z, half[0]], ZN)
    wyo1 = same(S_W + 17, WB.at[yo, z, half[0]], ZP)
    wzf0.wait_recv()
    wzf1.wait_recv()
    wzo0 = same(S_W + 18, WB.at[y, zo, half[1]], YN)
    wzo1 = same(S_W + 19, WB.at[y, zo, half[1]], YP)
    w3 = []
    for i, (copy, ref, dev) in enumerate(
        (
            (wyp0, WB.at[yp, zp, quart[0][0]], ZN),
            (wyp1, WB.at[yp, zn, quart[0][1]], ZP),
            (wzp0, WB.at[yp, zp, quart[1][0]], YN),
            (wzp1, WB.at[yn, zp, quart[1][1]], YP),
            (wyn0, WB.at[yn, zp, quart[0][0]], ZN),
            (wyn1, WB.at[yn, zn, quart[0][1]], ZP),
            (wzn0, WB.at[yp, zn, quart[1][0]], YN),
            (wzn1, WB.at[yn, zn, quart[1][1]], YP),
        )
    ):
        copy.wait_recv()
        w3.append(same(S_W + 20 + i, ref, dev))

    for copy in f3:
        copy.wait_recv()

    mean_of = jnp.full((WIDE, WIDE), 1.0 / WIDE, BF)

    def halves(a):
        high = a.astype(BF)
        return high, (a - high.astype(F32)).astype(BF)

    def row_mean(a):
        high, low = halves(a)
        return dot(high, mean_of) + dot(low, mean_of)

    def attend_head(h, _):
        hs = head_cols(h)
        att = ATT[:, hs] + jnp.exp(CC[h]) * dot(q[:, hs], ENT[h])
        r = lax.rsqrt(row_mean(att * att) + EPSILON)
        scaled = att * r
        ATT[:, hs] = scaled
        RN[h] = r
        MX[c, :, hs] = (scaled * gain[:, hs]).astype(BF)
        return 0

    lax.fori_loop(0, HEADS, attend_head, 0)
    mix = put(S_MIX, MX.at[c], MX.at[c], SIB)

    for i, (copy, ref, dev) in enumerate(
        (
            (wyo0, WB.at[yo, zp, quart[0][0]], ZN),
            (wyo1, WB.at[yo, zn, quart[0][1]], ZP),
            (wzo0, WB.at[yp, zo, quart[1][0]], YN),
            (wzo1, WB.at[yn, zo, quart[1][1]], YP),
        )
    ):
        copy.wait_recv()
        w3.append(same(S_W + 28 + i, ref, dev))

    def weight_term(xx):
        def tile(i, _):
            pair = lax.div(i, 2)
            n = lax.rem(i, 2)
            ms = pl.ds(pl.multiple_of(pair * 384, 384), 384)
            ns = pl.ds(pl.multiple_of(n * 512, 512), 512)
            term = dot_t0(OG[xx, pl.ds(0, ROWS), ms], MX[0, :, ns])
            term = term + dot_t0(OG[xx, pl.ds(ROWS, ROWS), ms], MX[1, :, ns])
            DW[xx, pl.ds(2 * pair, 2), :, ns] = term.reshape(2, UNIT, 512).astype(BF)
            return 0

        lax.fori_loop(0, 4, tile, 0)

    def delta_term(xx, first, half):
        def tile(n, _):
            ms = pl.ds(pl.multiple_of(half * ROWS, ROWS), ROWS)
            ns = pl.ds(pl.multiple_of(n * 256, 256), 256)
            term = dot(OG[xx, ms, :], WB[xx, :, :, ns].reshape(SPAN, 256))
            if first:
                ACC[ms, ns] = term
            else:
                ACC[ms, ns] += term
            return 0

        lax.fori_loop(0, 4, tile, 0)

    def add_to(target, *more):
        total = target.astype(F32)
        for term in more:
            total = total + term.astype(F32)
        return total.astype(BF)

    early = ((0, x), (1, xp), (2, xn))
    b1lo = make(S_RS + 0, DW.at[yo, :, quart[1][0]], R1B.at[0], YN)
    b1hi = make(S_RS + 1, DW.at[yo, :, quart[1][1]], R1B.at[1], YP)
    b2n = make(S_RS + 2, DW.at[yn, :, half[1]], R2B.at[0], YN)
    b2p = make(S_RS + 3, DW.at[yp, :, half[1]], R2B.at[1], YP)
    c1lo = make(S_RS + 4, DW.at[yo, z, quart[0][0]], R3.at[0, 0], YN)
    c1hi = make(S_RS + 5, DW.at[yo, z, quart[0][1]], R3.at[0, 1], YP)
    c2n = make(S_RS + 6, DW.at[yn, z, half[0]], R4.at[0, 0], YN)
    c2p = make(S_RS + 7, DW.at[yp, z, half[0]], R4.at[0, 1], YP)
    d1lo = make(S_RS + 8, DW.at[y, zo, quart[1][0]], R3.at[1, 0], ZN)
    d1hi = make(S_RS + 9, DW.at[y, zo, quart[1][1]], R3.at[1, 1], ZP)
    d2n = make(S_RS + 10, DW.at[y, zn, half[1]], R4.at[1, 0], ZN)
    d2p = make(S_RS + 11, DW.at[y, zp, half[1]], R4.at[1, 1], ZP)
    e1lo = make(S_E + 0, DW.at[xo, zo, half[0]], E1.at[0], ZN)
    e1hi = make(S_E + 1, DW.at[xo, zo, half[1]], E1.at[1], ZP)
    e2n = make(S_E + 2, DW.at[xo, zn], E2.at[0], ZN)
    e2p = make(S_E + 3, DW.at[xo, zp], E2.at[1], ZP)
    f1lo = make(S_E + 4, DW.at[xo, z, half[0]], E3.at[0], YN)
    f1hi = make(S_E + 5, DW.at[xo, z, half[1]], E3.at[1], YP)
    f2n = make(S_E + 6, DW.at[xo, z], E4.at[0], YN)
    f2p = make(S_E + 7, DW.at[xo, z], E4.at[1], YP)
    live += [e1lo, e1hi, e2n, e2p]
    a1 = {}
    a2 = {}

    def first_hop(j, xx):
        a1[j] = (
            put(S_A1 + 2 * j, DW.at[xx, zo, quart[0][0]], R1.at[0, j], ZN),
            put(S_A1 + 2 * j + 1, DW.at[xx, zo, quart[0][1]], R1.at[1, j], ZP),
        )

    def first_hop_y(xx):
        @pl.when(yo == xx)
        def _():
            b1lo.start()
            b1hi.start()

    def second_hop():
        for j, xx in early:
            a1[j][0].wait_recv()
            DW[xx, zn, quart[0][0]] = add_to(DW[xx, zn, quart[0][0]], R1[0, j])
            to_n = put(S_A2 + 2 * j, DW.at[xx, zn, half[0]], R2.at[0, j], ZN)
            a1[j][1].wait_recv()
            DW[xx, zp, quart[0][1]] = add_to(DW[xx, zp, quart[0][1]], R1[1, j])
            to_p = put(S_A2 + 2 * j + 1, DW.at[xx, zp, half[0]], R2.at[1, j], ZP)
            a2[j] = (to_n, to_p)

    def second_hop_y():
        @pl.when(yn != xo)
        def _():
            b1lo.wait_recv()
            for i in range(4):
                DW[yn, i, quart[1][0]] = add_to(DW[yn, i, quart[1][0]], R1B[0, i])
            b2n.start()

        @pl.when(yp != xo)
        def _():
            b1hi.wait_recv()
            for i in range(4):
                DW[yp, i, quart[1][1]] = add_to(DW[yp, i, quart[1][1]], R1B[1, i])
            b2p.start()

    def third_hop():
        for j, xx in early:
            a2[j][0].wait_recv()
            a2[j][1].wait_recv()
            DW[xx, z, half[0]] = add_to(DW[xx, z, half[0]], R2[0, j], R2[1, j])

        @pl.when(yo != xo)
        def _():
            c1lo.start()
            c1hi.start()

    def third_hop_y():
        @pl.when(y != xo)
        def _():
            b2n.wait_recv()
            b2p.wait_recv()
            for i in range(4):
                DW[y, i, half[1]] = add_to(DW[y, i, half[1]], R2B[0, i], R2B[1, i])
            d1lo.start()
            d1hi.start()

    def fourth_hop():
        @pl.when(yn != xo)
        def _():
            c1lo.wait_recv()
            DW[yn, z, quart[0][0]] = add_to(DW[yn, z, quart[0][0]], R3[0, 0])
            c2n.start()

        @pl.when(yp != xo)
        def _():
            c1hi.wait_recv()
            DW[yp, z, quart[0][1]] = add_to(DW[yp, z, quart[0][1]], R3[0, 1])
            c2p.start()

        @pl.when(y != xo)
        def _():
            d1lo.wait_recv()
            DW[y, zn, quart[1][0]] = add_to(DW[y, zn, quart[1][0]], R3[1, 0])
            d2n.start()
            d1hi.wait_recv()
            DW[y, zp, quart[1][1]] = add_to(DW[y, zp, quart[1][1]], R3[1, 1])
            d2p.start()

    def late_second_hop():
        e1lo.wait_recv()
        DW[xo, zn, half[0]] = add_to(DW[xo, zn, half[0]], E1[0])
        e2n.start()
        e1hi.wait_recv()
        DW[xo, zp, half[1]] = add_to(DW[xo, zp, half[1]], E1[1])
        e2p.start()

    def late_third_hop():
        e2n.wait_recv()
        e2p.wait_recv()
        for i in range(2):
            DW[xo, z, half[i]] = add_to(DW[xo, z, half[i]], E2[0, half[i]], E2[1, half[i]])

        @pl.when(yo == xo)
        def _():
            f1lo.start()
            f1hi.start()

    def late_fourth_hop():
        @pl.when(yn == xo)
        def _():
            f1lo.wait_recv()
            DW[xo, z, half[0]] = add_to(DW[xo, z, half[0]], E3[0])
            f2n.start()

        @pl.when(yp == xo)
        def _():
            f1hi.wait_recv()
            DW[xo, z, half[1]] = add_to(DW[xo, z, half[1]], E3[1])
            f2p.start()

    mix.wait_recv()
    weight_term(x)
    first_hop(0, x)
    first_hop_y(x)

    xr0.wait_recv()
    xr2 = put(S_X + 4, OG.at[xp, own_rows], OG.at[xp, own_rows], XN)
    xl0.wait_recv()
    xl2 = put(S_X + 5, OG.at[xn, sib_rows], OG.at[xn, sib_rows], XP)
    xr1.wait_recv()
    weight_term(xp)
    first_hop(1, xp)
    first_hop_y(xp)
    xl1.wait_recv()
    weight_term(xn)
    first_hop(2, xn)
    first_hop_y(xn)

    for copy in w3:
        copy.wait_recv()
    delta_term(x, True, o)
    delta_term(x, True, c)
    second_hop()
    delta_term(xp, False, o)
    delta_term(xp, False, c)
    second_hop_y()
    delta_term(xn, False, o)
    delta_term(xn, False, c)
    xr2.wait_recv()
    xl2.wait_recv()

    weight_term(xo)
    e1lo.start()
    e1hi.start()
    ods = []
    for m in range(2):

        def last_tile(n, _):
            ns = pl.ds(pl.multiple_of(n * 256, 256), 256)
            term = dot(OG[xo, sib_rows, :], WB[xo, :, :, ns].reshape(SPAN, 256))
            XO[:, ns] = (ACC[sib_rows, ns] + term).astype(BF)
            return 0

        lax.fori_loop(2 * m, 2 * m + 2, last_tile, 0)
        part = pl.ds(m * ROWS, ROWS)
        ods.append(put(S_OD + m, XO.at[:, part], XI.at[:, part], SIB))
    delta_term(xo, False, c)
    third_hop()
    for copy in ods:
        copy.wait_recv()

    def norm_back_head(h):
        hs = head_cols(h)
        delta = ACC[own_rows, hs] + XI[:, hs].astype(F32)
        scaled = ATT[:, hs]
        gg = delta * gain[:, hs]
        da = RN[h] * (gg - scaled * row_mean(gg * scaled))
        da, low = halves(da)
        DA[:, hs] = da
        DL[:, hs] = low
        qd = (q[:, hs].astype(F32) * jnp.exp(CC[h])).astype(BF)
        GS[h] = dot_t0(qd, da).astype(BF)

    def first_back(d):
        p, dev = mate(d)
        return make(S_B1 + d - 1, GS.at[p], GSI.at[grp], dev)

    def norm_back_step(d, _):
        norm_back_head(lax.rem(grp + d, 8))
        first_back(d).start()
        return 0

    lax.fori_loop(1, 8, norm_back_step, 0)
    norm_back_head(grp)
    GSI[grp] = GS[grp]
    b1 = [first_back(d) for d in range(1, 8)]
    live += b1

    late_second_hop()
    for copy in b1:
        copy.wait_recv()

    def chain_back(n, carry):
        i = 7 - n
        state, logs = carry
        log_i = join3(STI[i, pl.ds(WIDE, 16), :])
        LL[i] = state
        EP[i] = logs
        state = jnp.exp(log_i) * state + GSI[i].astype(F32)
        return state, logs + log_i

    row_back, _ = lax.fori_loop(
        0, 8, chain_back, (jnp.zeros((WIDE, WIDE), F32), jnp.zeros((1, WIDE), F32))
    )
    GR[...] = row_back.astype(BF)
    GRI[y] = GR[...]
    b2 = [
        put(S_B2 + d - 1, GR, GRI.at[y], at(turn(y, d), z, c)) for d in (1, 2, 3)
    ]

    def local_back_head(h, _):
        hs = head_cols(h)
        dk_blk = [None, None]
        dv_blk = [None, None]
        for tb in range(2):
            da = DA[blk(tb), hs]
            out = jnp.exp(CC[h, blk(tb), :]) * dot_t1(da, ENT[h])
            for sb in range(tb + 1):
                vs = v[blk(sb), hs]
                dp = dot_t1(da, vs) + dot_t1(DL[blk(tb), hs], vs)
                dp = (dp * decays(h, tb, sb)).astype(BF)
                out = out + dot(dp, k[blk(sb), hs])
                k_term = dot_t0(dp, q[blk(tb), hs])
                v_term = dot_t0(PB[h, blk(tb), blk(sb)], da)
                dk_blk[sb] = k_term if dk_blk[sb] is None else dk_blk[sb] + k_term
                dv_blk[sb] = v_term if dv_blk[sb] is None else dv_blk[sb] + v_term
            dq[blk(tb), hs] = out.astype(BF)
        for sb in range(2):
            ACC[blk(sb), hs] = dk_blk[sb]
            ACC[blk(2 + sb), hs] = dv_blk[sb]
        return 0

    lax.fori_loop(0, 4, local_back_head, 0)

    third_hop_y()
    for copy in b2:
        copy.wait_recv()
    carried_back = jnp.zeros((WIDE, WIDE), F32)
    for yy in (3, 2, 1):
        grown = jnp.exp(join3(RTI[yy, pl.ds(WIDE, 16), :])) * carried_back
        grown = grown + GRI[yy].astype(F32)
        carried_back = jnp.where(yy > y, grown, carried_back)

    def leave(i, _):
        GO[i] = (LL[i] + jnp.exp(EP[i]) * carried_back).astype(BF)
        return 0

    lax.fori_loop(0, 8, leave, 0)
    GG[grp] = GO[grp]
    b3 = []
    for d in range(1, 8):
        p, dev = mate(d)
        b3.append(put(S_B3 + d - 1, GO.at[p], GG.at[grp], dev))

    late_third_hop()
    lax.fori_loop(4, 8, local_back_head, 0)

    def last_head(h):
        hs = head_cols(h)
        total = CR[h, :, pl.ds(ROWS - WIDE, WIDE)][:, WIDE - 1 : WIDE]
        tail = jnp.exp(total - CC[h])
        dk[:, hs] = (ACC[pl.ds(0, ROWS), hs] + tail * dot_t1(v[:, hs], GG[h])).astype(BF)
        dv[:, hs] = (ACC[pl.ds(ROWS, ROWS), hs] + tail * dot(k[:, hs], GG[h])).astype(BF)

    fourth_hop()
    last_head(grp)

    def last_step(d, _):
        p = lax.rem(grp + 8 - d, 8)
        make(S_B3 + d - 1, GO.at[p], GG.at[grp], SIB).wait_recv()
        last_head(p)
        return 0

    late_fourth_hop()
    lax.fori_loop(1, 4, last_step, 0)
    lax.fori_loop(4, 8, last_step, 0)

    @pl.when(y != xo)
    def _():
        for i, (from_p, from_n) in enumerate(((c2n, c2p), (d2n, d2p))):
            from_p.wait_recv()
            from_n.wait_recv()
            dw[half[i], :] = (
                DW[y, z, half[i]].astype(F32) + R4[i, 0].astype(F32) + R4[i, 1].astype(F32)
            ) * SCALE

    @pl.when(y == xo)
    def _():
        f2n.wait_recv()
        f2p.wait_recv()
        for i in range(2):
            dw[half[i], :] = (
                DW[y, z, half[i]].astype(F32)
                + E4[0, half[i]].astype(F32)
                + E4[1, half[i]].astype(F32)
            ) * SCALE

    for place, copies in (
        (yo, (b1lo, b1hi, c1lo, c1hi)),
        (yn, (b2n, c2n)),
        (yp, (b2p, c2p)),
        (y, (d1lo, d1hi, d2n, d2p)),
    ):

        @pl.when(place != xo)
        def _():
            for copy in copies:
                copy.wait_send()

    for place, copies in ((yo, (f1lo, f1hi)), (yn, (f2n,)), (yp, (f2p,))):

        @pl.when(place == xo)
        def _():
            for copy in copies:
                copy.wait_send()

    for copy in live:
        copy.wait_send()


def body(query_rows, key_rows, value_rows, log_decay, norm_gain, out_weight, out_grad):
    vm = pltpu.VMEM
    scratch = [
        vm((4, 2 * ROWS, SPAN), BF),
        vm((ROWS, SPAN), BF),
        vm((4, 4, UNIT, COLS), BF),
        vm((2 * ROWS, COLS), F32),
        vm((ROWS, COLS), BF),
        vm((ROWS, COLS), BF),
        vm((2, ROWS, COLS), BF),
        vm((4, 4, UNIT, COLS), BF),
        vm((2, 3, QUART, COLS), BF),
        vm((2, 3, HALF, COLS), BF),
        vm((2, 2, QUART, COLS), BF),
        vm((2, 2, HALF, COLS), BF),
        vm((2, 4, QUART, COLS), BF),
        vm((2, 4, HALF, COLS), BF),
        vm((2, HALF, COLS), BF),
        vm((2, UNIT, COLS), BF),
        vm((2, HALF, COLS), BF),
        vm((2, UNIT, COLS), BF),
        vm((HEADS, ROWS, ROWS), BF),
        vm((ROWS, COLS), F32),
        vm((ROWS, COLS), BF),
        vm((ROWS, COLS), BF),
        vm((HEADS, ROWS, WIDE), F32),
        vm((HEADS, ROWS, WIDE), F32),
        vm((HEADS, 1, ROWS), F32),
        vm((8, WIDE + 16, WIDE), BF),
        vm((8, WIDE + 16, WIDE), BF),
        vm((WIDE + 16, WIDE), BF),
        vm((4, WIDE + 16, WIDE), BF),
        vm((8, WIDE, WIDE), BF),
        vm((8, WIDE, WIDE), BF),
        vm((8, WIDE, WIDE), F32),
        vm((8, 1, WIDE), F32),
        vm((8, WIDE, WIDE), BF),
        vm((8, WIDE, WIDE), BF),
        vm((WIDE, WIDE), BF),
        vm((4, WIDE, WIDE), BF),
        vm((8, WIDE, WIDE), BF),
        vm((8, WIDE, WIDE), BF),
        pltpu.SemaphoreType.DMA((S_ALL,)),
        pltpu.SemaphoreType.DMA((S_ALL,)),
    ]
    spec = pl.BlockSpec(memory_space=pltpu.VMEM)
    shapes = (
        jax.ShapeDtypeStruct((ROWS, COLS), BF),
        jax.ShapeDtypeStruct((ROWS, COLS), BF),
        jax.ShapeDtypeStruct((ROWS, COLS), BF),
        jax.ShapeDtypeStruct((UNIT, COLS), F32),
    )
    return pl.pallas_call(
        kernel,
        out_shape=shapes,
        in_specs=[spec] * 7,
        out_specs=(spec,) * 4,
        scratch_shapes=scratch,
        compiler_params=pltpu.CompilerParams(
            collective_id=0, has_side_effects=True, vmem_limit_bytes=62 * 2**20
        ),
    )(
        query_rows,
        key_rows,
        value_rows,
        log_decay,
        norm_gain.reshape(1, COLS),
        out_weight,
        out_grad,
    )


def solution(mesh):
    both = P("seq", "head")
    return jax.shard_map(
        body,
        mesh=mesh,
        in_specs=(both, both, both, P("head", "seq"), P("head"), both, both),
        out_specs=(both, both, both, both),
        check_vma=False,
    )
```
